128 devices in a mesh: state: 4 (over x), member: 32 (over z, y, core).
Axes of the slice: x: 4, y: 4, z: 4, core: 2. Of those that a mesh axis runs over, the one named last changes fastest.
Arguments:
- ensemble: bfloat16 [256, 131072], P('member', 'state'), may hold values from -8 to 8
- obs_count: int32 [256], replicated, may hold values from 0 to 11
Outputs:
- analysis: bfloat16 [256, 131072], P('member', 'state')
The draws below stay inside these ranges and needn't reach their ends.
All inputs are finite; a program needn't handle non-finite values.
Results may differ from the reference program's by a relative error of at most 0.0065.
Values may be sent and summed in bfloat16 or wider, within the bound.
A program may use at most 64 MiB of HBM per device.

```python
import math
import jax
import jax.numpy as jnp
from jax import lax

M = 256
SWEEPS = 20
STATE = 131072


def draw_ensemble(key, part):
    key = jax.random.fold_in(key, 7)
    subkeys = jax.random.split(key, 6)
    spread = 1.15
    column_norm = math.sqrt(math.sinh(2.0 * spread) / (2.0 * spread))
    column_scale = jnp.exp(jax.random.uniform(subkeys[0], (1, STATE), jnp.float32, -spread, spread)) / column_norm
    loadings = 0.35 * jax.random.truncated_normal(subkeys[1], -3.0, 3.0, (M, 4), jnp.float32)
    shapes = jax.random.truncated_normal(subkeys[2], -3.0, 3.0, (4, STATE), jnp.float32)
    field = loadings[:, 0:1] * shapes[0:1, :]
    for index in range(1, 4):
        field = field + loadings[:, index:index + 1] * shapes[index:index + 1, :]
    noise_level = 0.2 * jnp.exp(jax.random.uniform(subkeys[4], (M, 1), jnp.float32, -0.4, 0.4))
    noise = jax.random.truncated_normal(subkeys[5], -4.0, 4.0, (M, STATE), jnp.float32)
    values = column_scale * (field + noise_level * noise)
    return jnp.clip(values, -8.0, 8.0).astype(jnp.bfloat16)


def plant(entries, stream_key, smallest, largest):
    shape = entries.shape
    index_at = [jax.random.randint(jax.random.fold_in(stream_key, axis), (), 0, shape[axis]) for axis in range(len(shape))]
    entries = entries.at[tuple(index_at)].set(smallest)
    longest = shape.index(max(shape))
    index_at[longest] = (index_at[longest] + 1) % shape[longest]
    return entries.at[tuple(index_at)].set(largest)


def setup_inputs(seed: int = 0) -> dict:
    arg_keys = jax.random.split(jax.random.key(seed), 3)
    ensemble = draw_ensemble(jax.random.fold_in(arg_keys[2], 71), 0)
    obs_count = plant(jax.random.randint(arg_keys[1], (M,), 0, 12), jax.random.fold_in(arg_keys[1], 1), 0, 11).astype(jnp.int32)
    return {"ensemble": ensemble, "obs_count": obs_count}


def logsum(values, axis):
    top = jnp.max(values, axis=axis, keepdims=True)
    return jnp.squeeze(top, axis) + jnp.log(jnp.sum(jnp.exp(values - top), axis=axis))


def reference(ensemble, obs_count):
    gram = lax.dot_general(ensemble, ensemble, (((1,), (1,)), ((), ())), preferred_element_type=jnp.float32)
    norms = jnp.diagonal(gram)
    scale_cost = 16.0 / jnp.float32(STATE)
    cost = (norms[:, None] + norms[None, :] - 2.0 * gram) * scale_cost
    raw_weight = -2.0 * obs_count.astype(jnp.float32)
    logw = raw_weight - jnp.log(jnp.sum(jnp.exp(raw_weight)))
    f_pot = jnp.zeros((M,), jnp.float32)
    g_pot = jnp.zeros((M,), jnp.float32)
    for sweep in range(SWEEPS):
        f_pot = logw - logsum(g_pot[None, :] - cost, 1)
        g_pot = -jnp.log(jnp.float32(M)) - logsum(f_pot[:, None] - cost, 0)
    plan = (M * jnp.exp(f_pot[:, None] + g_pot[None, :] - cost)).astype(jnp.bfloat16)
    result = lax.dot_general(plan, ensemble, (((0,), (0,)), ((), ())), preferred_element_type=jnp.float32)
    return result.astype(jnp.bfloat16)
```

```python
import functools
import math

import jax
import jax.numpy as jnp
from jax import lax
from jax.experimental import pallas as pl
from jax.experimental.pallas import tpu as pltpu
from jax.sharding import PartitionSpec as P

SWEEPS = 20
MESH = pl.DeviceIdType.MESH
LOG2E = math.log2(math.e)


def member_peer(step, size):
    return lax.rem(lax.axis_index("member") + step, size)


def kernel(
    n_member, n_state, total,
    ens_ref, obs_ref, out_ref,
    slab, part, part_in, rows_in, gram, cost_ref, result,
    own_sem, send_sems, recv_sems,
):
    rows = ens_ref.shape[0]
    cols = ens_ref.shape[1] // n_member
    members = rows * n_member
    me = lax.axis_index("member")
    plane = lax.axis_index("state")

    barrier = pltpu.get_barrier_semaphore()

    def greet(step, carry):
        pl.semaphore_signal(
            barrier, inc=1, device_id={"member": member_peer(step, n_member)}, device_id_type=MESH
        )
        return carry

    lax.fori_loop(1, n_member, greet, 0)
    for step in range(1, n_state):
        pl.semaphore_signal(
            barrier, inc=1, device_id={"state": lax.rem(plane + step, n_state)}, device_id_type=MESH
        )
    pl.semaphore_wait(barrier, n_member - 1 + n_state - 1)

    def to_members(source, target, phase):
        def send(step, carry):
            peer = member_peer(step, n_member)
            pltpu.make_async_remote_copy(
                src_ref=source(peer),
                dst_ref=target,
                send_sem=send_sems.at[phase],
                recv_sem=recv_sems.at[phase],
                device_id={"member": peer},
                device_id_type=MESH,
            ).start()
            return carry

        lax.fori_loop(1, n_member, send, 0)

    def wait_for(ref, sem):
        pltpu.make_async_copy(ref, ref, sem).wait()

    own = pltpu.make_async_copy(
        ens_ref.at[:, pl.ds(pl.multiple_of(me * cols, cols), cols)], slab.at[me], own_sem
    )
    own.start()
    to_members(
        lambda peer: ens_ref.at[:, pl.ds(pl.multiple_of(peer * cols, cols), cols)], slab.at[me], 0
    )

    raw = -2.0 * obs_ref[...].astype(jnp.float32)
    logw_row = (raw - jnp.log(jnp.sum(jnp.exp(raw), axis=1, keepdims=True))) * LOG2E
    eye = lax.broadcasted_iota(jnp.int32, (members, members), 0) == lax.broadcasted_iota(
        jnp.int32, (members, members), 1
    )
    logw = jnp.sum(jnp.where(eye, logw_row, 0.0), axis=1, keepdims=True)

    own.wait()
    wait_for(slab.at[pl.ds(0, n_member - 1)], recv_sems.at[0])

    held = slab[...].reshape(members, cols)
    partial_gram = lax.dot_general(
        held, held, (((1,), (1,)), ((), ())), preferred_element_type=jnp.float32
    )
    part[...] = partial_gram.reshape(n_member, rows, members)

    part_in[me] = part[me]
    to_members(lambda peer: part.at[peer], part_in.at[me], 1)
    wait_for(part.at[pl.ds(0, n_member - 1)], recv_sems.at[1])
    rows_in[plane] = jnp.sum(part_in[...], axis=0)
    for step in range(1, n_state):
        pltpu.make_async_remote_copy(
            src_ref=rows_in.at[plane],
            dst_ref=rows_in.at[plane],
            send_sem=send_sems.at[2],
            recv_sem=recv_sems.at[2],
            device_id={"state": lax.rem(plane + step, n_state)},
            device_id_type=MESH,
        ).start()
    wait_for(rows_in.at[pl.ds(0, n_state - 1)], recv_sems.at[2])
    gram[me] = jnp.sum(rows_in[...], axis=0)
    to_members(lambda peer: gram.at[me], gram.at[me], 3)
    wait_for(gram.at[pl.ds(0, n_member - 1)], recv_sems.at[3])

    whole = gram[...].reshape(members, members)
    diagonal = jnp.where(eye, whole, 0.0)
    norm_col = jnp.sum(diagonal, axis=1, keepdims=True)
    norm_row = jnp.sum(diagonal, axis=0, keepdims=True)
    cost = (norm_col + norm_row - 2.0 * whole) * (16.0 / total * LOG2E)
    cost_ref[...] = cost
    log_count = math.log2(members)

    def sweep(index, carry):
        f_pot, g_pot = carry
        cost = cost_ref[...]
        sums = jnp.sum(jnp.exp2(f_pot + g_pot - cost), axis=1, keepdims=True)
        f_pot = f_pot + logw - jnp.log2(sums)
        sums = jnp.sum(jnp.exp2(f_pot + g_pot - cost), axis=0, keepdims=True)
        g_pot = g_pot - log_count - jnp.log2(sums)
        return (f_pot, g_pot)

    f_pot, g_pot = lax.fori_loop(
        0,
        SWEEPS,
        sweep,
        (jnp.zeros((members, 1), jnp.float32), jnp.zeros((1, members), jnp.float32)),
    )
    cost = cost_ref[...]
    plan = jnp.exp2(f_pot + g_pot - cost + log_count).astype(jnp.bfloat16)
    analysis = lax.dot_general(
        plan, slab[...].reshape(members, cols), (((0,), (0,)), ((), ())),
        preferred_element_type=jnp.float32,
    )
    result[...] = analysis.reshape(n_member, rows, cols).astype(jnp.bfloat16)

    mine = out_ref.at[:, pl.ds(pl.multiple_of(me * cols, cols), cols)]
    own = pltpu.make_async_copy(result.at[me], mine, own_sem)
    own.start()
    to_members(lambda peer: result.at[peer], mine, 4)
    own.wait()
    wait_for(out_ref.at[:, pl.ds(0, (n_member - 1) * cols)], recv_sems.at[4])

    wait_for(slab.at[pl.ds(0, n_member - 1)], send_sems.at[0])
    wait_for(part.at[pl.ds(0, n_member - 1)], send_sems.at[1])
    wait_for(rows_in.at[pl.ds(0, n_state - 1)], send_sems.at[2])
    wait_for(gram.at[pl.ds(0, n_member - 1)], send_sems.at[3])
    wait_for(result.at[pl.ds(0, n_member - 1)], send_sems.at[4])


def per_device(n_member, n_state, ensemble, obs_count):
    rows, width = ensemble.shape
    members, cols = rows * n_member, width // n_member
    return pl.pallas_call(
        functools.partial(kernel, n_member, n_state, width * n_state),
        out_shape=jax.ShapeDtypeStruct((rows, width), jnp.bfloat16),
        in_specs=[pl.BlockSpec(memory_space=pl.ANY), pl.BlockSpec(memory_space=pltpu.VMEM)],
        out_specs=pl.BlockSpec(memory_space=pl.ANY),
        scratch_shapes=[
            pltpu.VMEM((n_member, rows, cols), jnp.bfloat16),
            pltpu.VMEM((n_member, rows, members), jnp.float32),
            pltpu.VMEM((n_member, rows, members), jnp.float32),
            pltpu.VMEM((n_state, rows, members), jnp.float32),
            pltpu.VMEM((n_member, rows, members), jnp.float32),
            pltpu.VMEM((members, members), jnp.float32),
            pltpu.VMEM((n_member, rows, cols), jnp.bfloat16),
            pltpu.SemaphoreType.DMA,
            pltpu.SemaphoreType.DMA((5,)),
            pltpu.SemaphoreType.DMA((5,)),
        ],
        compiler_params=pltpu.CompilerParams(
            collective_id=0, has_side_effects=True, vmem_limit_bytes=32 * 1024 * 1024
        ),
    )(ensemble, obs_count.reshape(1, members))


def solution(mesh):
    body = functools.partial(per_device, mesh.shape["member"], mesh.shape["state"])
    return jax.shard_map(
        body, mesh=mesh, in_specs=(P("member", "state"), P()), out_specs=P("member", "state"),
        check_vma=False,
    )
```

```python
import functools
import math

import jax
import jax.numpy as jnp
from jax import lax
from jax.experimental import pallas as pl
from jax.experimental.pallas import tpu as pltpu
from jax.sharding import PartitionSpec as P

SWEEPS = 20
MESH = pl.DeviceIdType.MESH
LOG2E = math.log2(math.e)


def hops(offset):
    return sum(min(step, 4 - step) for step in offset[:2])


OFFSETS = sorted(
    ((z, y, c) for z in range(4) for y in range(4) for c in range(2) if (z, y, c) != (0, 0, 0)),
    key=lambda offset: -hops(offset),
)


def member_peers():
    me = lax.axis_index("member")
    z, y, c = lax.div(me, 8), lax.rem(lax.div(me, 2), 4), lax.rem(me, 2)
    return [
        lax.rem(z + dz, 4) * 8 + lax.rem(y + dy, 4) * 2 + lax.rem(c + dc, 2)
        for dz, dy, dc in OFFSETS
    ]


def kernel(
    n_member, n_state, total,
    ens_ref, obs_ref, out_ref,
    slab, obs, part, part_in, rows_in, dist, cost_ref, result,
    own_sems, send_sems, recv_sems,
):
    rows = ens_ref.shape[0]
    cols = ens_ref.shape[1] // n_member
    members = rows * n_member
    half = members // 2
    me = lax.axis_index("member")
    plane = lax.axis_index("state")
    peers = member_peers()
    planes = [lax.rem(plane + step, n_state) for step in range(1, n_state)]

    barrier = pltpu.get_barrier_semaphore()
    for peer in peers:
        pl.semaphore_signal(barrier, inc=1, device_id={"member": peer}, device_id_type=MESH)
    for other in planes:
        pl.semaphore_signal(barrier, inc=1, device_id={"state": other}, device_id_type=MESH)

    def column_block(ref, index):
        return ref.at[:, pl.ds(pl.multiple_of(index * cols, cols), cols)]

    own_obs = pltpu.make_async_copy(obs_ref, obs, own_sems.at[0])
    own_obs.start()
    own_block = pltpu.make_async_copy(column_block(ens_ref, me), slab.at[me], own_sems.at[1])
    own_block.start()
    pl.semaphore_wait(barrier, n_member - 1 + n_state - 1)

    def send(source, target, phase, device):
        pltpu.make_async_remote_copy(
            src_ref=source,
            dst_ref=target,
            send_sem=send_sems.at[phase],
            recv_sem=recv_sems.at[phase],
            device_id=device,
            device_id_type=MESH,
        ).start()

    def wait_for(ref, sem):
        pltpu.make_async_copy(ref, ref, sem).wait()

    for peer in peers:
        send(column_block(ens_ref, peer), slab.at[me], 0, {"member": peer})

    own_obs.wait()
    raw = -2.0 * obs[...].astype(jnp.float32)
    logw = (raw - jnp.log(jnp.sum(jnp.exp(raw), axis=1, keepdims=True))) * LOG2E
    row = lax.broadcasted_iota(jnp.int32, (members, members), 0)
    column = lax.broadcasted_iota(jnp.int32, (members, members), 1)
    eye = row == column
    above = row[:half, :half] < column[:half, :half]

    own_block.wait()
    wait_for(slab.at[pl.ds(0, n_member - 1)], recv_sems.at[0])

    held = slab[...].reshape(members, cols)
    gram = lax.dot_general(
        held, held, (((1,), (1,)), ((), ())), preferred_element_type=jnp.float32
    )
    diagonal = jnp.where(eye, gram, 0.0)
    norm_col = jnp.sum(diagonal, axis=1, keepdims=True)
    norm_row = jnp.sum(diagonal, axis=0, keepdims=True)
    apart = norm_col + norm_row - 2.0 * gram
    folded = jnp.where(above, apart[:half, :half], apart[half:, half:])
    part[: n_member // 2] = folded.reshape(n_member // 2, rows, half)
    part[n_member // 2 :] = apart[:half, half:].reshape(n_member // 2, rows, half)

    for peer in peers:
        send(part.at[peer], part_in.at[me], 1, {"member": peer})
    part_in[me] = part[me]
    wait_for(part.at[pl.ds(0, n_member - 1)], recv_sems.at[1])
    rows_in[plane] = jnp.sum(part_in[...], axis=0)
    for other in planes:
        send(rows_in.at[plane], rows_in.at[plane], 2, {"state": other})
    wait_for(rows_in.at[pl.ds(0, n_state - 1)], recv_sems.at[2])
    dist[me] = jnp.sum(rows_in[...], axis=0)
    for peer in peers:
        send(dist.at[me], dist.at[me], 3, {"member": peer})
    wait_for(dist.at[pl.ds(0, n_member - 1)], recv_sems.at[3])

    scale_cost = 16.0 / total * LOG2E
    folded = dist[: n_member // 2].reshape(half, half) * scale_cost
    across = dist[n_member // 2 :].reshape(half, half) * scale_cost
    first = jnp.where(above, folded, 0.0)
    second = folded - first
    cost_ref[:half, :half] = first + first.T
    cost_ref[half:, half:] = second + second.T
    cost_ref[:half, half:] = across
    cost_ref[half:, :half] = across.T
    log_count = math.log2(members)

    def sweep(index, carry):
        f_pot, g_pot = carry
        cost = cost_ref[...]
        sums = jnp.sum(jnp.exp2(g_pot + f_pot - cost), axis=0, keepdims=True)
        f_pot = f_pot + logw - jnp.log2(sums)
        sums = jnp.sum(jnp.exp2(g_pot + f_pot - cost), axis=1, keepdims=True)
        g_pot = g_pot - log_count - jnp.log2(sums)
        return (f_pot, g_pot)

    f_pot, g_pot = lax.fori_loop(
        0,
        SWEEPS,
        sweep,
        (jnp.zeros((1, members), jnp.float32), jnp.zeros((members, 1), jnp.float32)),
    )
    plan = jnp.exp2(g_pot + f_pot - cost_ref[...] + log_count).astype(jnp.bfloat16)
    analysis = lax.dot_general(
        plan, slab[...].reshape(members, cols), (((1,), (0,)), ((), ())),
        preferred_element_type=jnp.float32,
    )
    result[...] = analysis.reshape(n_member, rows, cols).astype(jnp.bfloat16)

    mine = column_block(out_ref, me)
    for peer in peers:
        send(result.at[peer], mine, 4, {"member": peer})
    own_block = pltpu.make_async_copy(result.at[me], mine, own_sems.at[1])
    own_block.start()

    wait_for(slab.at[pl.ds(0, n_member - 1)], send_sems.at[0])
    wait_for(part.at[pl.ds(0, n_member - 1)], send_sems.at[1])
    wait_for(rows_in.at[pl.ds(0, n_state - 1)], send_sems.at[2])
    wait_for(dist.at[pl.ds(0, n_member - 1)], send_sems.at[3])
    own_block.wait()
    wait_for(result.at[pl.ds(0, n_member - 1)], send_sems.at[4])
    wait_for(out_ref.at[:, pl.ds(0, (n_member - 1) * cols)], recv_sems.at[4])


def per_device(n_member, n_state, ensemble, obs_count):
    rows, width = ensemble.shape
    members, cols = rows * n_member, width // n_member
    half = members // 2
    return pl.pallas_call(
        functools.partial(kernel, n_member, n_state, width * n_state),
        out_shape=jax.ShapeDtypeStruct((rows, width), jnp.bfloat16),
        in_specs=[pl.BlockSpec(memory_space=pl.ANY), pl.BlockSpec(memory_space=pl.ANY)],
        out_specs=pl.BlockSpec(memory_space=pl.ANY),
        scratch_shapes=[
            pltpu.VMEM((n_member, rows, cols), jnp.bfloat16),
            pltpu.VMEM((1, members), jnp.int32),
            pltpu.VMEM((n_member, rows, half), jnp.float32),
            pltpu.VMEM((n_member, rows, half), jnp.float32),
            pltpu.VMEM((n_state, rows, half), jnp.float32),
            pltpu.VMEM((n_member, rows, half), jnp.float32),
            pltpu.VMEM((members, members), jnp.float32),
            pltpu.VMEM((n_member, rows, cols), jnp.bfloat16),
            pltpu.SemaphoreType.DMA((2,)),
            pltpu.SemaphoreType.DMA((5,)),
            pltpu.SemaphoreType.DMA((5,)),
        ],
        compiler_params=pltpu.CompilerParams(
            collective_id=0, has_side_effects=True, vmem_limit_bytes=60 * 1024 * 1024
        ),
    )(ensemble, obs_count.reshape(1, members))


def solution(mesh):
    body = functools.partial(per_device, mesh.shape["member"], mesh.shape["state"])
    return jax.shard_map(
        body, mesh=mesh, in_specs=(P("member", "state"), P()), out_specs=P("member", "state"),
        check_vma=False,
    )
```

```python
import functools
import math

import jax
import jax.numpy as jnp
from jax import lax
from jax.experimental import pallas as pl
from jax.experimental.pallas import tpu as pltpu
from jax.sharding import PartitionSpec as P

SWEEPS = 20
MESH = pl.DeviceIdType.MESH
LOG2E = math.log2(math.e)


def hops(offset):
    return sum(min(step, 4 - step) for step in offset[:3])


OFFSETS = sorted(
    (
        (x, z, y, c)
        for x in range(4) for z in range(4) for y in range(4) for c in range(2)
        if (x, z, y, c) != (0, 0, 0, 0)
    ),
    key=lambda offset: -hops(offset),
)


def others():
    plane, me = lax.axis_index("state"), lax.axis_index("member")
    z, y, c = lax.div(me, 8), lax.rem(lax.div(me, 2), 4), lax.rem(me, 2)
    everyone, members = [], []
    for dx, dz, dy, dc in OFFSETS:
        member = lax.rem(z + dz, 4) * 8 + lax.rem(y + dy, 4) * 2 + lax.rem(c + dc, 2)
        everyone.append((lax.rem(plane + dx, 4), member))
        if dx == 0:
            members.append(member)
    return everyone, members


def kernel(
    n_member, n_state, total,
    ens_ref, obs_ref, out_ref,
    slab, obs, part, part_in, dist, cost_ref, result,
    own_sems, send_sems, recv_sems, ready_sem,
):
    rows = ens_ref.shape[0]
    cols = ens_ref.shape[1] // n_member
    members = rows * n_member
    half = members // 2
    me = lax.axis_index("member")
    plane = lax.axis_index("state")
    everyone, peers = others()
    n_all = n_member * n_state
    rank = plane * n_member + me
    planes = [lax.rem(plane + step, n_state) for step in range(1, n_state)]

    barrier = pltpu.get_barrier_semaphore()
    for peer in peers:
        pl.semaphore_signal(barrier, inc=1, device_id={"member": peer}, device_id_type=MESH)
    for other in planes:
        pl.semaphore_signal(barrier, inc=1, device_id={"state": other}, device_id_type=MESH)

    def column_block(ref, index):
        return ref.at[:, pl.ds(pl.multiple_of(index * cols, cols), cols)]

    own_obs = pltpu.make_async_copy(obs_ref, obs, own_sems.at[0])
    own_obs.start()
    own_block = pltpu.make_async_copy(column_block(ens_ref, me), slab.at[me], own_sems.at[1])
    own_block.start()
    pl.semaphore_wait(barrier, n_member - 1 + n_state - 1)
    for other in planes:
        pl.semaphore_signal(ready_sem, inc=1, device_id={"state": other}, device_id_type=MESH)

    def send(source, target, phase, device):
        pltpu.make_async_remote_copy(
            src_ref=source,
            dst_ref=target,
            send_sem=send_sems.at[phase],
            recv_sem=recv_sems.at[phase],
            device_id=device,
            device_id_type=MESH,
        ).start()

    def wait_for(ref, sem):
        pltpu.make_async_copy(ref, ref, sem).wait()

    for peer in peers:
        send(column_block(ens_ref, peer), slab.at[me], 0, {"member": peer})

    own_obs.wait()
    raw = -2.0 * obs[...].astype(jnp.float32)
    logw = (raw - jnp.log(jnp.sum(jnp.exp(raw), axis=1, keepdims=True))) * LOG2E
    row = lax.broadcasted_iota(jnp.int32, (members, members), 0)
    column = lax.broadcasted_iota(jnp.int32, (members, members), 1)
    eye = row == column
    above = row[:half, :half] < column[:half, :half]

    own_block.wait()
    wait_for(slab.at[pl.ds(0, n_member - 1)], recv_sems.at[0])

    held = slab[...].reshape(members, cols)
    gram = lax.dot_general(
        held, held, (((1,), (1,)), ((), ())), preferred_element_type=jnp.float32
    )
    diagonal = jnp.where(eye, gram, 0.0)
    norm_col = jnp.sum(diagonal, axis=1, keepdims=True)
    norm_row = jnp.sum(diagonal, axis=0, keepdims=True)
    apart = norm_col + norm_row - 2.0 * gram
    folded = jnp.where(above, apart[:half, :half], apart[half:, half:])
    part[: n_all // 2] = folded.reshape(n_all // 2, 2, half)
    part[n_all // 2 :] = apart[:half, half:].reshape(n_all // 2, 2, half)

    pl.semaphore_wait(ready_sem, n_state - 1)
    for other, peer in everyone:
        send(
            part.at[other * n_member + peer], part_in.at[rank], 1,
            {"state": other, "member": peer},
        )
    part_in[rank] = part[rank]
    wait_for(part.at[pl.ds(0, n_all - 1)], recv_sems.at[1])
    dist[rank] = jnp.sum(part_in[...], axis=0)
    for other, peer in everyone:
        send(dist.at[rank], dist.at[rank], 2, {"state": other, "member": peer})
    wait_for(dist.at[pl.ds(0, n_all - 1)], recv_sems.at[2])

    scale_cost = 16.0 / total * LOG2E
    folded = dist[: n_all // 2].reshape(half, half) * scale_cost
    across = dist[n_all // 2 :].reshape(half, half) * scale_cost
    first = jnp.where(above, folded, 0.0)
    second = folded - first
    cost_ref[:half, :half] = first + first.T
    cost_ref[half:, half:] = second + second.T
    cost_ref[:half, half:] = across
    cost_ref[half:, :half] = across.T
    log_count = math.log2(members)

    def sweep(index, carry):
        f_pot, g_pot = carry
        cost = cost_ref[...]
        sums = jnp.sum(jnp.exp2(g_pot + f_pot - cost), axis=0, keepdims=True)
        f_pot = f_pot + logw - jnp.log2(sums)
        sums = jnp.sum(jnp.exp2(g_pot + f_pot - cost), axis=1, keepdims=True)
        g_pot = g_pot - log_count - jnp.log2(sums)
        return (f_pot, g_pot)

    f_pot, g_pot = lax.fori_loop(
        0,
        SWEEPS,
        sweep,
        (jnp.zeros((1, members), jnp.float32), jnp.zeros((members, 1), jnp.float32)),
    )
    plan = jnp.exp2(g_pot + f_pot - cost_ref[...] + log_count).astype(jnp.bfloat16)
    analysis = lax.dot_general(
        plan, slab[...].reshape(members, cols), (((1,), (0,)), ((), ())),
        preferred_element_type=jnp.float32,
    )
    result[...] = analysis.reshape(n_member, rows, cols).astype(jnp.bfloat16)

    mine = column_block(out_ref, me)
    for peer in peers:
        send(result.at[peer], mine, 3, {"member": peer})
    own_block = pltpu.make_async_copy(result.at[me], mine, own_sems.at[1])
    own_block.start()

    wait_for(slab.at[pl.ds(0, n_member - 1)], send_sems.at[0])
    wait_for(part.at[pl.ds(0, n_all - 1)], send_sems.at[1])
    wait_for(dist.at[pl.ds(0, n_all - 1)], send_sems.at[2])
    own_block.wait()
    wait_for(result.at[pl.ds(0, n_member - 1)], send_sems.at[3])
    wait_for(out_ref.at[:, pl.ds(0, (n_member - 1) * cols)], recv_sems.at[3])


def per_device(n_member, n_state, ensemble, obs_count):
    rows, width = ensemble.shape
    members, cols = rows * n_member, width // n_member
    half, n_all = members // 2, n_member * n_state
    return pl.pallas_call(
        functools.partial(kernel, n_member, n_state, width * n_state),
        out_shape=jax.ShapeDtypeStruct((rows, width), jnp.bfloat16),
        in_specs=[pl.BlockSpec(memory_space=pl.ANY), pl.BlockSpec(memory_space=pl.ANY)],
        out_specs=pl.BlockSpec(memory_space=pl.ANY),
        scratch_shapes=[
            pltpu.VMEM((n_member, rows, cols), jnp.bfloat16),
            pltpu.VMEM((1, members), jnp.int32),
            pltpu.VMEM((n_all, 2, half), jnp.float32),
            pltpu.VMEM((n_all, 2, half), jnp.float32),
            pltpu.VMEM((n_all, 2, half), jnp.float32),
            pltpu.VMEM((members, members), jnp.float32),
            pltpu.VMEM((n_member, rows, cols), jnp.bfloat16),
            pltpu.SemaphoreType.DMA((2,)),
            pltpu.SemaphoreType.DMA((4,)),
            pltpu.SemaphoreType.DMA((4,)),
            pltpu.SemaphoreType.REGULAR,
        ],
        compiler_params=pltpu.CompilerParams(
            collective_id=0, has_side_effects=True, vmem_limit_bytes=53 * 1024 * 1024
        ),
    )(ensemble, obs_count.reshape(1, members))


def solution(mesh):
    body = functools.partial(per_device, mesh.shape["member"], mesh.shape["state"])
    return jax.shard_map(
        body, mesh=mesh, in_specs=(P("member", "state"), P()), out_specs=P("member", "state"),
        check_vma=False,
    )
```

```python
import functools
import math

import jax
import jax.numpy as jnp
from jax import lax
from jax.experimental import pallas as pl
from jax.experimental.pallas import tpu as pltpu
from jax.sharding import PartitionSpec as P

SWEEPS = 20
MESH = pl.DeviceIdType.MESH
LOG2E = math.log2(math.e)


def hops(offset):
    return sum(min(step, 4 - step) for step in offset[:3])


OFFSETS = sorted(
    (
        (x, z, y, c)
        for x in range(4) for z in range(4) for y in range(4) for c in range(2)
        if (x, z, y, c) != (0, 0, 0, 0)
    ),
    key=lambda offset: -hops(offset),
)


def others():
    plane, me = lax.axis_index("state"), lax.axis_index("member")
    z, y, c = lax.div(me, 8), lax.rem(lax.div(me, 2), 4), lax.rem(me, 2)
    everyone, members = [], []
    for dx, dz, dy, dc in OFFSETS:
        member = lax.rem(z + dz, 4) * 8 + lax.rem(y + dy, 4) * 2 + lax.rem(c + dc, 2)
        everyone.append((lax.rem(plane + dx, 4), member))
        if dx == 0:
            members.append(member)
    return everyone, members


def kernel(
    n_member, n_state, total,
    ens_ref, obs_ref, out_ref,
    slab, obs, part, part_in, dist, cost_ref, result,
    own_sems, send_sems, recv_sems, ready_sem,
):
    rows = ens_ref.shape[0]
    cols = ens_ref.shape[1] // n_member
    members = rows * n_member
    half = members // 2
    me = lax.axis_index("member")
    plane = lax.axis_index("state")
    everyone, peers = others()
    n_all = n_member * n_state
    rank = plane * n_member + me
    planes = [lax.rem(plane + step, n_state) for step in range(1, n_state)]

    barrier = pltpu.get_barrier_semaphore()
    for peer in peers:
        pl.semaphore_signal(barrier, inc=1, device_id={"member": peer}, device_id_type=MESH)
    for other in planes:
        pl.semaphore_signal(barrier, inc=1, device_id={"state": other}, device_id_type=MESH)

    def column_block(ref, index):
        return ref.at[:, pl.ds(pl.multiple_of(index * cols, cols), cols)]

    own_obs = pltpu.make_async_copy(obs_ref, obs, own_sems.at[0])
    own_obs.start()
    own_block = pltpu.make_async_copy(column_block(ens_ref, me), slab.at[me], own_sems.at[1])
    own_block.start()
    pl.semaphore_wait(barrier, n_member - 1 + n_state - 1)
    for other in planes:
        pl.semaphore_signal(ready_sem, inc=1, device_id={"state": other}, device_id_type=MESH)

    def send(source, target, phase, device):
        pltpu.make_async_remote_copy(
            src_ref=source,
            dst_ref=target,
            send_sem=send_sems.at[phase],
            recv_sem=recv_sems.at[phase],
            device_id=device,
            device_id_type=MESH,
        ).start()

    def wait_for(ref, sem):
        pltpu.make_async_copy(ref, ref, sem).wait()

    for peer in peers:
        send(column_block(ens_ref, peer), slab.at[me], 0, {"member": peer})

    own_obs.wait()
    raw = -2.0 * obs[...].astype(jnp.float32)
    logw = (raw - jnp.log(jnp.sum(jnp.exp(raw), axis=1, keepdims=True))) * LOG2E
    row = lax.broadcasted_iota(jnp.int32, (members, members), 0)
    column = lax.broadcasted_iota(jnp.int32, (members, members), 1)
    eye = row == column
    above = row[:half, :half] < column[:half, :half]

    own_block.wait()
    wait_for(slab.at[pl.ds(0, n_member - 1)], recv_sems.at[0])

    held = slab[...].reshape(members, cols)
    gram = lax.dot_general(
        held, held, (((1,), (1,)), ((), ())), preferred_element_type=jnp.float32
    )
    diagonal = jnp.where(eye, gram, 0.0)
    norm_col = jnp.sum(diagonal, axis=1, keepdims=True)
    norm_row = jnp.sum(diagonal, axis=0, keepdims=True)
    apart = norm_col + norm_row - 2.0 * gram
    folded = jnp.where(above, apart[:half, :half], apart[half:, half:])
    part[: n_all // 2] = folded.reshape(n_all // 2, 2, half)
    part[n_all // 2 :] = apart[:half, half:].reshape(n_all // 2, 2, half)

    pl.semaphore_wait(ready_sem, n_state - 1)
    for other, peer in everyone:
        send(
            part.at[other * n_member + peer], part_in.at[rank], 1,
            {"state": other, "member": peer},
        )
    part_in[rank] = part[rank]
    wait_for(part.at[pl.ds(0, n_all - 1)], recv_sems.at[1])
    dist[rank] = jnp.sum(part_in[...], axis=0)
    for other, peer in everyone:
        send(dist.at[rank], dist.at[rank], 2, {"state": other, "member": peer})
    wait_for(dist.at[pl.ds(0, n_all - 1)], recv_sems.at[2])

    scale_cost = 16.0 / total * LOG2E
    folded = dist[: n_all // 2].reshape(half, half) * scale_cost
    across = dist[n_all // 2 :].reshape(half, half) * scale_cost
    first = jnp.where(above, folded, 0.0)
    second = folded - first
    cost_ref[:half, :half] = first + first.T
    cost_ref[half:, half:] = second + second.T
    cost_ref[:half, half:] = across
    cost_ref[half:, :half] = across.T
    log_count = math.log2(members)

    weight = jnp.exp2(logw)

    def sweep(index, carry):
        f_pot, g_pot = carry
        scaled = jnp.exp2(g_pot + f_pot - cost_ref[...])
        sums = jnp.sum(scaled, axis=0, keepdims=True)
        f_pot = f_pot + logw - jnp.log2(sums)
        sums = jnp.sum(scaled * (weight / sums), axis=1, keepdims=True)
        g_pot = g_pot - log_count - jnp.log2(sums)
        return (f_pot, g_pot)

    f_pot, g_pot = lax.fori_loop(
        0,
        SWEEPS,
        sweep,
        (jnp.zeros((1, members), jnp.float32), jnp.zeros((members, 1), jnp.float32)),
        unroll=4,
    )
    plan = jnp.exp2(g_pot + f_pot - cost_ref[...] + log_count).astype(jnp.bfloat16)
    analysis = lax.dot_general(
        plan, slab[...].reshape(members, cols), (((1,), (0,)), ((), ())),
        preferred_element_type=jnp.float32,
    )
    result[...] = analysis.reshape(n_member, rows, cols).astype(jnp.bfloat16)

    mine = column_block(out_ref, me)
    for peer in peers:
        send(result.at[peer], mine, 3, {"member": peer})
    own_block = pltpu.make_async_copy(result.at[me], mine, own_sems.at[1])
    own_block.start()

    wait_for(slab.at[pl.ds(0, n_member - 1)], send_sems.at[0])
    wait_for(part.at[pl.ds(0, n_all - 1)], send_sems.at[1])
    wait_for(dist.at[pl.ds(0, n_all - 1)], send_sems.at[2])
    own_block.wait()
    wait_for(result.at[pl.ds(0, n_member - 1)], send_sems.at[3])
    wait_for(out_ref.at[:, pl.ds(0, (n_member - 1) * cols)], recv_sems.at[3])


def per_device(n_member, n_state, ensemble, obs_count):
    rows, width = ensemble.shape
    members, cols = rows * n_member, width // n_member
    half, n_all = members // 2, n_member * n_state
    return pl.pallas_call(
        functools.partial(kernel, n_member, n_state, width * n_state),
        out_shape=jax.ShapeDtypeStruct((rows, width), jnp.bfloat16),
        in_specs=[pl.BlockSpec(memory_space=pl.ANY), pl.BlockSpec(memory_space=pl.ANY)],
        out_specs=pl.BlockSpec(memory_space=pl.ANY),
        scratch_shapes=[
            pltpu.VMEM((n_member, rows, cols), jnp.bfloat16),
            pltpu.VMEM((1, members), jnp.int32),
            pltpu.VMEM((n_all, 2, half), jnp.float32),
            pltpu.VMEM((n_all, 2, half), jnp.float32),
            pltpu.VMEM((n_all, 2, half), jnp.float32),
            pltpu.VMEM((members, members), jnp.float32),
            pltpu.VMEM((n_member, rows, cols), jnp.bfloat16),
            pltpu.SemaphoreType.DMA((2,)),
            pltpu.SemaphoreType.DMA((4,)),
            pltpu.SemaphoreType.DMA((4,)),
            pltpu.SemaphoreType.REGULAR,
        ],
        compiler_params=pltpu.CompilerParams(
            collective_id=0, has_side_effects=True, vmem_limit_bytes=53 * 1024 * 1024
        ),
    )(
        pltpu.with_memory_space_constraint(ensemble, pltpu.HBM),
        pltpu.with_memory_space_constraint(obs_count.reshape(1, members), pltpu.HBM),
    )


def solution(mesh):
    body = functools.partial(per_device, mesh.shape["member"], mesh.shape["state"])
    return jax.shard_map(
        body, mesh=mesh, in_specs=(P("member", "state"), P()), out_specs=P("member", "state"),
        check_vma=False,
    )
```

```python
import functools
import math

import jax
import jax.numpy as jnp
from jax import lax
from jax.experimental import pallas as pl
from jax.experimental.pallas import tpu as pltpu
from jax.sharding import PartitionSpec as P

SWEEPS = 20
MESH = pl.DeviceIdType.MESH
LOG2E = math.log2(math.e)


def hops(offset):
    return sum(min(step, 4 - step) for step in offset[:3])


OFFSETS = sorted(
    (
        (x, z, y, c)
        for x in range(4) for z in range(4) for y in range(4) for c in range(2)
        if (x, z, y, c) != (0, 0, 0, 0)
    ),
    key=lambda offset: -hops(offset),
)


NEAR = (
    ((2, 0), (1, 1), (1, 3), (1, 0), (3, 0), (0, 1), (0, 3), (0, 0)),
    ((0, 2), (3, 3), (3, 1), (1, 0), (3, 0), (0, 1), (0, 3), (0, 0)),
)
FAR_CHIPS = 3


def near_chips():
    me = lax.axis_index("member")
    z, y, c = lax.div(me, 8), lax.rem(lax.div(me, 2), 4), lax.rem(me, 2)
    return [
        lax.rem(z + a[0] + c * (b[0] - a[0]) + 4, 4) * 4 + lax.rem(y + a[1] + c * (b[1] - a[1]) + 4, 4)
        for a, b in zip(*NEAR)
    ]


def antipode(member):
    z, y, c = lax.div(member, 8), lax.rem(lax.div(member, 2), 4), lax.rem(member, 2)
    return lax.rem(z + 2, 4) * 8 + lax.rem(y + 2, 4) * 2 + c


def others():
    plane, me = lax.axis_index("state"), lax.axis_index("member")
    z, y, c = lax.div(me, 8), lax.rem(lax.div(me, 2), 4), lax.rem(me, 2)
    everyone, members = [], []
    for dx, dz, dy, dc in OFFSETS:
        member = lax.rem(z + dz, 4) * 8 + lax.rem(y + dy, 4) * 2 + lax.rem(c + dc, 2)
        everyone.append((lax.rem(plane + dx, 4), member))
        if dx == 0:
            members.append(member)
    return everyone, members


def kernel(
    n_member, n_state, total,
    ens_ref, obs_ref, out_ref,
    slab, twin, obs, part, part_in, dist, cost_ref, plan_ref, result,
    own_sems, send_sems, recv_sems, ready_sem,
):
    rows = ens_ref.shape[0]
    cols = ens_ref.shape[1] // n_member
    members = rows * n_member
    half = members // 2
    me = lax.axis_index("member")
    plane = lax.axis_index("state")
    everyone, peers = others()
    n_all = n_member * n_state
    rank = plane * n_member + me
    planes = [lax.rem(plane + step, n_state) for step in range(1, n_state)]

    barrier = pltpu.get_barrier_semaphore()
    for peer in peers:
        pl.semaphore_signal(barrier, inc=1, device_id={"member": peer}, device_id_type=MESH)
    for other in planes:
        pl.semaphore_signal(barrier, inc=1, device_id={"state": other}, device_id_type=MESH)

    def column_block(ref, index):
        return ref.at[:, pl.ds(pl.multiple_of(index * cols, cols), cols)]

    own_obs = pltpu.make_async_copy(obs_ref, obs, own_sems.at[0])
    own_obs.start()
    far = antipode(me)
    own_block = pltpu.make_async_copy(column_block(ens_ref, me), slab.at[me], own_sems.at[1])
    own_block.start()
    own_twin = pltpu.make_async_copy(column_block(ens_ref, far), twin.at[me], own_sems.at[2])
    own_twin.start()
    pl.semaphore_wait(barrier, n_member - 1 + n_state - 1)
    for other in planes:
        pl.semaphore_signal(ready_sem, inc=1, device_id={"state": other}, device_id_type=MESH)

    def send(source, target, phase, device):
        pltpu.make_async_remote_copy(
            src_ref=source,
            dst_ref=target,
            send_sem=send_sems.at[phase],
            recv_sem=recv_sems.at[phase],
            device_id=device,
            device_id_type=MESH,
        ).start()

    def wait_for(ref, sem):
        pltpu.make_async_copy(ref, ref, sem).wait()

    for peer in peers:
        send(column_block(ens_ref, peer), slab.at[me], 0, {"member": peer})

    own_obs.wait()
    raw = -2.0 * obs[...].astype(jnp.float32)
    logw = (raw - jnp.log(jnp.sum(jnp.exp(raw), axis=1, keepdims=True))) * LOG2E
    row = lax.broadcasted_iota(jnp.int32, (members, members), 0)
    column = lax.broadcasted_iota(jnp.int32, (members, members), 1)
    eye = row == column
    above = row[:half, :half] < column[:half, :half]

    own_block.wait()
    wait_for(slab.at[pl.ds(0, n_member - 1)], recv_sems.at[0])

    held = slab[...].reshape(members, cols)
    gram = lax.dot_general(
        held, held, (((1,), (1,)), ((), ())), preferred_element_type=jnp.float32
    )
    diagonal = jnp.where(eye, gram, 0.0)
    norm_col = jnp.sum(diagonal, axis=1, keepdims=True)
    norm_row = jnp.sum(diagonal, axis=0, keepdims=True)
    apart = norm_col + norm_row - 2.0 * gram
    folded = jnp.where(above, apart[:half, :half], apart[half:, half:])
    part[: n_all // 2] = folded.reshape(n_all // 2, 2, half)
    part[n_all // 2 :] = apart[:half, half:].reshape(n_all // 2, 2, half)

    pl.semaphore_wait(ready_sem, n_state - 1)
    for other, peer in everyone:
        send(
            part.at[other * n_member + peer], part_in.at[rank], 1,
            {"state": other, "member": peer},
        )
    for peer in peers[::-1]:
        send(column_block(ens_ref, antipode(peer)), twin.at[me], 4, {"member": peer})
    part_in[rank] = part[rank]
    wait_for(part.at[pl.ds(0, n_all - 1)], recv_sems.at[1])
    dist[rank] = jnp.sum(part_in[...], axis=0)
    for other, peer in everyone:
        send(dist.at[rank], dist.at[rank], 2, {"state": other, "member": peer})

    wait_for(dist.at[pl.ds(0, n_all - 1)], recv_sems.at[2])

    scale_cost = 16.0 / total * LOG2E
    folded = dist[: n_all // 2].reshape(half, half) * scale_cost
    across = dist[n_all // 2 :].reshape(half, half) * scale_cost
    first = jnp.where(above, folded, 0.0)
    second = folded - first
    cost_ref[:half, :half] = first + first.T
    cost_ref[half:, half:] = second + second.T
    cost_ref[:half, half:] = across
    cost_ref[half:, :half] = across.T
    log_count = math.log2(members)

    weight = jnp.exp2(logw)

    def sweep(index, carry):
        f_pot, g_pot = carry
        scaled = jnp.exp2(g_pot + f_pot - cost_ref[...])
        sums = jnp.sum(scaled, axis=0, keepdims=True)
        f_pot = f_pot + logw - jnp.log2(sums)
        sums = jnp.sum(scaled * (weight / sums), axis=1, keepdims=True)
        g_pot = g_pot - log_count - jnp.log2(sums)
        return (f_pot, g_pot)

    f_pot, g_pot = lax.fori_loop(
        0,
        SWEEPS,
        sweep,
        (jnp.zeros((1, members), jnp.float32), jnp.zeros((members, 1), jnp.float32)),
        unroll=4,
    )
    plan = jnp.exp2(g_pot + f_pot - cost_ref[...] + log_count).astype(jnp.bfloat16)
    n_chips = n_member // 2
    plan_ref[...] = plan.reshape(n_chips, 2 * rows, members)
    own_twin.wait()
    wait_for(twin.at[pl.ds(0, n_member - 1)], recv_sems.at[4])

    chips = near_chips()
    served = len(chips)
    core = lax.rem(me, 2)
    own_sets = []
    for start, stop in ((0, FAR_CHIPS), (FAR_CHIPS, served)):
        mine = jnp.concatenate([plan_ref[chip] for chip in chips[start:stop]], axis=0)
        for which, (columns, owner) in enumerate(((slab, me), (twin, far))):
            analysis = lax.dot_general(
                mine, columns[...].reshape(members, cols), (((1,), (0,)), ((), ())),
                preferred_element_type=jnp.float32,
            )
            result[which, 2 * start : 2 * stop] = analysis.reshape(
                2 * (stop - start), rows, cols
            ).astype(jnp.bfloat16)
            target = column_block(out_ref, owner)
            for place in range(start, stop):
                if place < served - 1:
                    for side in range(2):
                        send(
                            result.at[which, 2 * place + side], target, 3,
                            {"member": chips[place] * 2 + side},
                        )
                else:
                    send(
                        result.at[which, 2 * place + 1 - core], target, 3, {"member": me + 1 - 2 * core}
                    )
                    copy = pltpu.make_async_copy(
                        result.at[which, 2 * place + core], target, own_sems.at[1 + which]
                    )
                    copy.start()
                    own_sets.append(copy)

    wait_for(slab.at[pl.ds(0, n_member - 1)], send_sems.at[0])
    wait_for(part.at[pl.ds(0, n_all - 1)], send_sems.at[1])
    wait_for(dist.at[pl.ds(0, n_all - 1)], send_sems.at[2])
    wait_for(twin.at[pl.ds(0, n_member - 1)], send_sems.at[4])
    for copy in own_sets:
        copy.wait()
    wait_for(out_ref.at[:, pl.ds(0, (n_member - 2) * cols)], send_sems.at[3])
    wait_for(out_ref.at[:, pl.ds(0, (n_member - 2) * cols)], recv_sems.at[3])


def per_device(n_member, n_state, ensemble, obs_count):
    rows, width = ensemble.shape
    members, cols = rows * n_member, width // n_member
    half, n_all = members // 2, n_member * n_state
    return pl.pallas_call(
        functools.partial(kernel, n_member, n_state, width * n_state),
        out_shape=jax.ShapeDtypeStruct((rows, width), jnp.bfloat16),
        in_specs=[pl.BlockSpec(memory_space=pl.ANY), pl.BlockSpec(memory_space=pl.ANY)],
        out_specs=pl.BlockSpec(memory_space=pl.ANY),
        scratch_shapes=[
            pltpu.VMEM((n_member, rows, cols), jnp.bfloat16),
            pltpu.VMEM((n_member, rows, cols), jnp.bfloat16),
            pltpu.VMEM((1, members), jnp.int32),
            pltpu.VMEM((n_all, 2, half), jnp.float32),
            pltpu.VMEM((n_all, 2, half), jnp.float32),
            pltpu.VMEM((n_all, 2, half), jnp.float32),
            pltpu.VMEM((members, members), jnp.float32),
            pltpu.VMEM((n_member // 2, 2 * rows, members), jnp.bfloat16),
            pltpu.VMEM((2, n_member // 2, rows, cols), jnp.bfloat16),
            pltpu.SemaphoreType.DMA((3,)),
            pltpu.SemaphoreType.DMA((5,)),
            pltpu.SemaphoreType.DMA((5,)),
            pltpu.SemaphoreType.REGULAR,
        ],
        compiler_params=pltpu.CompilerParams(
            collective_id=0, has_side_effects=True, vmem_limit_bytes=53 * 1024 * 1024
        ),
    )(
        pltpu.with_memory_space_constraint(ensemble, pltpu.HBM),
        pltpu.with_memory_space_constraint(obs_count.reshape(1, members), pltpu.HBM),
    )


def solution(mesh):
    body = functools.partial(per_device, mesh.shape["member"], mesh.shape["state"])
    return jax.shard_map(
        body, mesh=mesh, in_specs=(P("member", "state"), P()), out_specs=P("member", "state"),
        check_vma=False,
    )
```

```python
import functools
import math

import jax
import jax.numpy as jnp
from jax import lax
from jax.experimental import pallas as pl
from jax.experimental.pallas import tpu as pltpu
from jax.sharding import PartitionSpec as P

SWEEPS = 20
MESH = pl.DeviceIdType.MESH
LOG2E = math.log2(math.e)


def nearness(offset):
    steps = [min(step, 4 - step) for step in offset[:3]]
    return (-sum(steps), max(steps), offset[3])


OFFSETS = sorted(
    (
        (x, z, y, c)
        for x in range(4) for z in range(4) for y in range(4) for c in range(2)
        if (x, z, y, c) != (0, 0, 0, 0)
    ),
    key=nearness,
)


NEAR = (
    ((2, 0), (1, 1), (1, 3), (1, 0), (3, 0), (0, 1), (0, 3), (0, 0)),
    ((0, 2), (3, 3), (3, 1), (1, 0), (3, 0), (0, 1), (0, 3), (0, 0)),
)
FAR_CHIPS = 3


def near_chips():
    me = lax.axis_index("member")
    z, y, c = lax.div(me, 8), lax.rem(lax.div(me, 2), 4), lax.rem(me, 2)
    return [
        lax.rem(z + a[0] + c * (b[0] - a[0]) + 4, 4) * 4 + lax.rem(y + a[1] + c * (b[1] - a[1]) + 4, 4)
        for a, b in zip(*NEAR)
    ]


def antipode(member):
    z, y, c = lax.div(member, 8), lax.rem(lax.div(member, 2), 4), lax.rem(member, 2)
    return lax.rem(z + 2, 4) * 8 + lax.rem(y + 2, 4) * 2 + c


def others():
    plane, me = lax.axis_index("state"), lax.axis_index("member")
    z, y, c = lax.div(me, 8), lax.rem(lax.div(me, 2), 4), lax.rem(me, 2)
    planes = [lax.rem(plane + step, 4) for step in range(4)]
    layers = [lax.rem(z + step, 4) * 8 for step in range(4)]
    lines = [lax.rem(y + step, 4) * 2 for step in range(4)]
    cores = [c, 1 - c]
    members = {
        (dz, dy, dc): layers[dz] + lines[dy] + cores[dc]
        for dz in range(4) for dy in range(4) for dc in range(2)
    }
    everyone = [(planes[dx], members[dz, dy, dc]) for dx, dz, dy, dc in OFFSETS]
    peers = [members[dz, dy, dc] for dx, dz, dy, dc in OFFSETS if dx == 0]
    return everyone, peers


def kernel(
    n_member, n_state, total,
    ens_ref, obs_ref, out_ref,
    own, slab, twin, obs, part, part_in, dist, cost_ref, plan_ref, result,
    own_sems, send_sems, recv_sems, ready_sem,
):
    rows = ens_ref.shape[0]
    cols = ens_ref.shape[1] // n_member
    members = rows * n_member
    half = members // 2
    me = lax.axis_index("member")
    plane = lax.axis_index("state")
    everyone, peers = others()
    n_all = n_member * n_state
    rank = plane * n_member + me
    planes = [lax.rem(plane + step, n_state) for step in range(1, n_state)]

    barrier = pltpu.get_barrier_semaphore()
    for peer in peers:
        pl.semaphore_signal(barrier, inc=1, device_id={"member": peer}, device_id_type=MESH)
    for other in planes:
        pl.semaphore_signal(barrier, inc=1, device_id={"state": other}, device_id_type=MESH)

    def column_block(ref, index):
        return ref.at[:, pl.ds(pl.multiple_of(index * cols, cols), cols)]

    own_obs = pltpu.make_async_copy(obs_ref, obs, own_sems.at[0])
    own_obs.start()
    staged = pltpu.make_async_copy(ens_ref, own, own_sems.at[3])
    staged.start()
    far = antipode(me)
    own_block = pltpu.make_async_copy(column_block(ens_ref, me), slab.at[me], own_sems.at[1])
    own_block.start()
    own_twin = pltpu.make_async_copy(column_block(ens_ref, far), twin.at[me], own_sems.at[2])
    own_twin.start()
    pl.semaphore_wait(barrier, n_member - 1 + n_state - 1)
    for other in planes:
        pl.semaphore_signal(ready_sem, inc=1, device_id={"state": other}, device_id_type=MESH)

    def send(source, target, phase, device):
        pltpu.make_async_remote_copy(
            src_ref=source,
            dst_ref=target,
            send_sem=send_sems.at[phase],
            recv_sem=recv_sems.at[phase],
            device_id=device,
            device_id_type=MESH,
        ).start()

    def wait_for(ref, sem):
        pltpu.make_async_copy(ref, ref, sem).wait()

    staged.wait()
    for peer in peers:
        send(column_block(own, peer), slab.at[me], 0, {"member": peer})

    own_obs.wait()
    raw = -2.0 * obs[...].astype(jnp.float32)
    logw = (raw - jnp.log(jnp.sum(jnp.exp(raw), axis=1, keepdims=True))) * LOG2E
    row = lax.broadcasted_iota(jnp.int32, (members, members), 0)
    column = lax.broadcasted_iota(jnp.int32, (members, members), 1)
    eye = row == column
    above = row[:half, :half] < column[:half, :half]

    own_block.wait()
    wait_for(slab.at[pl.ds(0, n_member - 1)], recv_sems.at[0])

    held = slab[...].reshape(members, cols)
    gram = lax.dot_general(
        held, held, (((1,), (1,)), ((), ())), preferred_element_type=jnp.float32
    )
    diagonal = jnp.where(eye, gram, 0.0)
    norm_col = jnp.sum(diagonal, axis=1, keepdims=True)
    norm_row = jnp.sum(diagonal, axis=0, keepdims=True)
    apart = norm_col + norm_row - 2.0 * gram
    folded = jnp.where(above, apart[:half, :half], apart[half:, half:])
    part[: n_all // 2] = folded.reshape(n_all // 2, 2, half)
    part[n_all // 2 :] = apart[:half, half:].reshape(n_all // 2, 2, half)

    pl.semaphore_wait(ready_sem, n_state - 1)
    for other, peer in everyone:
        send(
            part.at[other * n_member + peer], part_in.at[rank], 1,
            {"state": other, "member": peer},
        )
    for peer in peers[:8:-1]:
        send(column_block(own, antipode(peer)), twin.at[me], 4, {"member": peer})
    part_in[rank] = part[rank]
    wait_for(part.at[pl.ds(0, n_all - 1)], recv_sems.at[1])
    sums = jnp.sum(part_in[...].reshape(members // 8, 8, half), axis=0)
    dist[rank] = sums[0:2] + sums[2:4] + (sums[4:6] + sums[6:8])
    for other, peer in everyone:
        send(dist.at[rank], dist.at[rank], 2, {"state": other, "member": peer})

    for peer in peers[8::-1]:
        send(column_block(own, antipode(peer)), twin.at[me], 4, {"member": peer})
    wait_for(dist.at[pl.ds(0, n_all - 1)], recv_sems.at[2])

    scale_cost = 16.0 / total * LOG2E
    folded = dist[: n_all // 2].reshape(half, half) * scale_cost
    across = dist[n_all // 2 :].reshape(half, half) * scale_cost
    first = jnp.where(above, folded, 0.0)
    second = folded - first
    cost_ref[:half, :half] = first + first.T
    cost_ref[half:, half:] = second + second.T
    cost_ref[:half, half:] = across
    cost_ref[half:, :half] = across.T
    log_count = math.log2(members)

    weight = jnp.exp2(logw)

    def sweep(index, carry):
        f_pot, g_pot = carry
        scaled = jnp.exp2(g_pot + f_pot - cost_ref[...])
        sums = jnp.sum(scaled, axis=0, keepdims=True)
        f_pot = f_pot + logw - jnp.log2(sums)
        sums = jnp.sum(scaled * (weight / sums), axis=1, keepdims=True)
        g_pot = g_pot - log_count - jnp.log2(sums)
        return (f_pot, g_pot)

    f_pot, g_pot = lax.fori_loop(
        0,
        SWEEPS,
        sweep,
        (jnp.zeros((1, members), jnp.float32), jnp.zeros((members, 1), jnp.float32)),
        unroll=4,
    )
    plan = jnp.exp2(g_pot + f_pot - cost_ref[...] + log_count).astype(jnp.bfloat16)
    n_chips = n_member // 2
    plan_ref[...] = plan.reshape(n_chips, 2 * rows, members)
    own_twin.wait()
    wait_for(twin.at[pl.ds(0, n_member - 1)], recv_sems.at[4])

    chips = near_chips()
    served = len(chips)
    core = lax.rem(me, 2)
    own_sets = []
    mine = jnp.concatenate([plan_ref[chip] for chip in chips], axis=0)
    for which, (columns, owner) in enumerate(((slab, me), (twin, far))):
        analysis = lax.dot_general(
            mine, columns[...].reshape(members, cols), (((1,), (0,)), ((), ())),
            preferred_element_type=jnp.float32,
        )
        result[which] = analysis.reshape(2 * served, rows, cols).astype(jnp.bfloat16)
        target = column_block(out_ref, owner)
        for place, chip in enumerate(chips[:-1]):
            for side in range(2):
                send(result.at[which, 2 * place + side], target, 3, {"member": chip * 2 + side})
        last = 2 * (served - 1)
        send(result.at[which, last + 1 - core], target, 3, {"member": me + 1 - 2 * core})
        copy = pltpu.make_async_copy(result.at[which, last + core], target, own_sems.at[1 + which])
        copy.start()
        own_sets.append(copy)

    wait_for(slab.at[pl.ds(0, n_member - 1)], send_sems.at[0])
    wait_for(part.at[pl.ds(0, n_all - 1)], send_sems.at[1])
    wait_for(dist.at[pl.ds(0, n_all - 1)], send_sems.at[2])
    wait_for(twin.at[pl.ds(0, n_member - 1)], send_sems.at[4])
    for copy in own_sets:
        copy.wait()
    wait_for(out_ref.at[:, pl.ds(0, (n_member - 2) * cols)], send_sems.at[3])
    wait_for(out_ref.at[:, pl.ds(0, (n_member - 2) * cols)], recv_sems.at[3])


def per_device(n_member, n_state, ensemble, obs_count):
    rows, width = ensemble.shape
    members, cols = rows * n_member, width // n_member
    half, n_all = members // 2, n_member * n_state
    return pl.pallas_call(
        functools.partial(kernel, n_member, n_state, width * n_state),
        out_shape=jax.ShapeDtypeStruct((rows, width), jnp.bfloat16),
        in_specs=[pl.BlockSpec(memory_space=pl.ANY), pl.BlockSpec(memory_space=pl.ANY)],
        out_specs=pl.BlockSpec(memory_space=pl.ANY),
        scratch_shapes=[
            pltpu.VMEM((rows, width), jnp.bfloat16),
            pltpu.VMEM((n_member, rows, cols), jnp.bfloat16),
            pltpu.VMEM((n_member, rows, cols), jnp.bfloat16),
            pltpu.VMEM((1, members), jnp.int32),
            pltpu.VMEM((n_all, 2, half), jnp.float32),
            pltpu.VMEM((n_all, 2, half), jnp.float32),
            pltpu.VMEM((n_all, 2, half), jnp.float32),
            pltpu.VMEM((members, members), jnp.float32),
            pltpu.VMEM((n_member // 2, 2 * rows, members), jnp.bfloat16),
            pltpu.VMEM((2, n_member // 2, rows, cols), jnp.bfloat16),
            pltpu.SemaphoreType.DMA((4,)),
            pltpu.SemaphoreType.DMA((5,)),
            pltpu.SemaphoreType.DMA((5,)),
            pltpu.SemaphoreType.REGULAR,
        ],
        compiler_params=pltpu.CompilerParams(
            collective_id=0, has_side_effects=True, vmem_limit_bytes=53 * 1024 * 1024
        ),
    )(
        pltpu.with_memory_space_constraint(ensemble, pltpu.HBM),
        pltpu.with_memory_space_constraint(obs_count.reshape(1, members), pltpu.HBM),
    )


def solution(mesh):
    body = functools.partial(per_device, mesh.shape["member"], mesh.shape["state"])
    return jax.shard_map(
        body, mesh=mesh, in_specs=(P("member", "state"), P()), out_specs=P("member", "state"),
        check_vma=False,
    )
```

```python
import functools
import math

import jax
import jax.numpy as jnp
from jax import lax
from jax.experimental import pallas as pl
from jax.experimental.pallas import tpu as pltpu
from jax.sharding import PartitionSpec as P

SWEEPS = 20
MESH = pl.DeviceIdType.MESH
LOG2E = math.log2(math.e)


def nearness(offset):
    steps = [min(step, 4 - step) for step in offset[:3]]
    return (-sum(steps), max(steps), offset[3])


OFFSETS = sorted(
    (
        (x, z, y, c)
        for x in range(4) for z in range(4) for y in range(4) for c in range(2)
        if (x, z, y, c) != (0, 0, 0, 0)
    ),
    key=nearness,
)


NEAR = (
    ((2, 0), (1, 1), (1, 3), (1, 0), (3, 0), (0, 1), (0, 3), (0, 0)),
    ((0, 2), (3, 3), (3, 1), (1, 0), (3, 0), (0, 1), (0, 3), (0, 0)),
)
FAR_CHIPS = 3


def near_chips():
    me = lax.axis_index("member")
    z, y, c = lax.div(me, 8), lax.rem(lax.div(me, 2), 4), lax.rem(me, 2)
    return [
        lax.rem(z + a[0] + c * (b[0] - a[0]) + 4, 4) * 4 + lax.rem(y + a[1] + c * (b[1] - a[1]) + 4, 4)
        for a, b in zip(*NEAR)
    ]


def antipode(member):
    z, y, c = lax.div(member, 8), lax.rem(lax.div(member, 2), 4), lax.rem(member, 2)
    return lax.rem(z + 2, 4) * 8 + lax.rem(y + 2, 4) * 2 + c


def others():
    plane, me = lax.axis_index("state"), lax.axis_index("member")
    z, y, c = lax.div(me, 8), lax.rem(lax.div(me, 2), 4), lax.rem(me, 2)
    planes = [lax.rem(plane + step, 4) for step in range(4)]
    layers = [lax.rem(z + step, 4) * 8 for step in range(4)]
    lines = [lax.rem(y + step, 4) * 2 for step in range(4)]
    cores = [c, 1 - c]
    members = {
        (dz, dy, dc): layers[dz] + lines[dy] + cores[dc]
        for dz in range(4) for dy in range(4) for dc in range(2)
    }
    everyone = [(planes[dx], members[dz, dy, dc]) for dx, dz, dy, dc in OFFSETS]
    peers = [members[dz, dy, dc] for dx, dz, dy, dc in OFFSETS if dx == 0]
    return everyone, peers


def kernel(
    n_member, n_state, total,
    ens_ref, obs_ref, out_ref,
    own, slab, twin, obs, part, part_in, dist, cost_ref, plan_ref, result,
    own_sems, send_sems, recv_sems, ready_sem,
):
    rows = ens_ref.shape[0]
    cols = ens_ref.shape[1] // n_member
    members = rows * n_member
    half = members // 2
    me = lax.axis_index("member")
    plane = lax.axis_index("state")
    everyone, peers = others()
    n_all = n_member * n_state
    rank = plane * n_member + me
    planes = [lax.rem(plane + step, n_state) for step in range(1, n_state)]

    barrier = pltpu.get_barrier_semaphore()
    for peer in peers:
        pl.semaphore_signal(barrier, inc=1, device_id={"member": peer}, device_id_type=MESH)
    for other in planes:
        pl.semaphore_signal(barrier, inc=1, device_id={"state": other}, device_id_type=MESH)

    def column_block(ref, index):
        return ref.at[:, pl.ds(pl.multiple_of(index * cols, cols), cols)]

    own_obs = pltpu.make_async_copy(obs_ref, obs, own_sems.at[0])
    own_obs.start()
    staged = pltpu.make_async_copy(ens_ref, own, own_sems.at[3])
    staged.start()
    far = antipode(me)
    own_block = pltpu.make_async_copy(column_block(ens_ref, me), slab.at[me], own_sems.at[1])
    own_block.start()
    own_twin = pltpu.make_async_copy(column_block(ens_ref, far), twin.at[me], own_sems.at[2])
    own_twin.start()
    pl.semaphore_wait(barrier, n_member - 1 + n_state - 1)
    for other in planes:
        pl.semaphore_signal(ready_sem, inc=1, device_id={"state": other}, device_id_type=MESH)

    def send(source, target, phase, device):
        pltpu.make_async_remote_copy(
            src_ref=source,
            dst_ref=target,
            send_sem=send_sems.at[phase],
            recv_sem=recv_sems.at[phase],
            device_id=device,
            device_id_type=MESH,
        ).start()

    def wait_for(ref, sem):
        pltpu.make_async_copy(ref, ref, sem).wait()

    staged.wait()
    for peer in peers:
        send(column_block(own, peer), slab.at[me], 0, {"member": peer})

    own_obs.wait()
    raw = -2.0 * obs[...].astype(jnp.float32)
    logw = (raw - jnp.log(jnp.sum(jnp.exp(raw), axis=1, keepdims=True))) * LOG2E
    row = lax.broadcasted_iota(jnp.int32, (members, members), 0)
    column = lax.broadcasted_iota(jnp.int32, (members, members), 1)
    eye = row == column
    above = row[:half, :half] < column[:half, :half]

    own_block.wait()
    wait_for(slab.at[pl.ds(0, n_member - 1)], recv_sems.at[0])

    held = slab[...].reshape(members, cols)
    gram = lax.dot_general(
        held, held, (((1,), (1,)), ((), ())), preferred_element_type=jnp.float32
    )
    diagonal = jnp.where(eye, gram, 0.0)
    norm_col = jnp.sum(diagonal, axis=1, keepdims=True)
    norm_row = jnp.sum(diagonal, axis=0, keepdims=True)
    apart = norm_col + norm_row - 2.0 * gram
    folded = jnp.where(above, apart[:half, :half], apart[half:, half:])
    part[: n_all // 2] = folded.reshape(n_all // 2, 2, half)
    part[n_all // 2 :] = apart[:half, half:].reshape(n_all // 2, 2, half)

    pl.semaphore_wait(ready_sem, n_state - 1)
    for other, peer in everyone:
        send(
            part.at[other * n_member + peer], part_in.at[rank], 1,
            {"state": other, "member": peer},
        )
    for peer in peers[:8:-1]:
        send(column_block(own, antipode(peer)), twin.at[me], 4, {"member": peer})
    part_in[rank] = part[rank]
    wait_for(part.at[pl.ds(0, n_all - 1)], recv_sems.at[1])
    sums = jnp.sum(part_in[...].reshape(members // 8, 8, half), axis=0)
    dist[rank] = sums[0:2] + sums[2:4] + (sums[4:6] + sums[6:8])
    for other in range(n_state):
        for peer in peers:
            send(dist.at[rank], dist.at[rank], 2, {"state": other, "member": peer})

        @pl.when(plane != other)
        def _():
            send(dist.at[rank], dist.at[rank], 2, {"state": other, "member": me})

    for peer in peers[8::-1]:
        send(column_block(own, antipode(peer)), twin.at[me], 4, {"member": peer})
    wait_for(dist.at[pl.ds(0, n_all - 1)], recv_sems.at[2])

    scale_cost = 16.0 / total * LOG2E
    folded = dist[: n_all // 2].reshape(half, half) * scale_cost
    across = dist[n_all // 2 :].reshape(half, half) * scale_cost
    first = jnp.where(above, folded, 0.0)
    second = folded - first
    cost_ref[:half, :half] = first + first.T
    cost_ref[half:, half:] = second + second.T
    cost_ref[:half, half:] = across
    cost_ref[half:, :half] = across.T
    log_count = math.log2(members)

    weight = jnp.exp2(logw)

    def sweep(index, carry):
        f_pot, g_pot = carry
        scaled = jnp.exp2(g_pot + f_pot - cost_ref[...])
        sums = jnp.sum(scaled, axis=0, keepdims=True)
        f_pot = f_pot + logw - jnp.log2(sums)
        sums = jnp.sum(scaled * (weight / sums), axis=1, keepdims=True)
        g_pot = g_pot - log_count - jnp.log2(sums)
        return (f_pot, g_pot)

    f_pot, g_pot = lax.fori_loop(
        0,
        SWEEPS,
        sweep,
        (jnp.zeros((1, members), jnp.float32), jnp.zeros((members, 1), jnp.float32)),
        unroll=4,
    )
    plan = jnp.exp2(g_pot + f_pot - cost_ref[...] + log_count).astype(jnp.bfloat16)
    n_chips = n_member // 2
    plan_ref[...] = plan.reshape(n_chips, 2 * rows, members)
    own_twin.wait()
    wait_for(twin.at[pl.ds(0, n_member - 1)], recv_sems.at[4])

    chips = near_chips()
    served = len(chips)
    core = lax.rem(me, 2)
    mine = jnp.concatenate([plan_ref[chip] for chip in chips], axis=0)
    for which, columns in enumerate((slab, twin)):
        analysis = lax.dot_general(
            mine, columns[...].reshape(members, cols), (((1,), (0,)), ((), ())),
            preferred_element_type=jnp.float32,
        )
        result[which] = analysis.reshape(2 * served, rows, cols).astype(jnp.bfloat16)

    def serve(place):
        for which, owner in enumerate((me, far)):
            target = column_block(out_ref, owner)
            if place < served - 1:
                for side in range(2):
                    send(
                        result.at[which, 2 * place + side], target, 3,
                        {"member": chips[place] * 2 + side},
                    )
            else:
                send(
                    result.at[which, 2 * place + 1 - core], target, 3, {"member": me + 1 - 2 * core}
                )

    for turn in range(4):
        for place in range(served):
            pl.when(lax.div(chips[place], 4) == turn)(functools.partial(serve, place))
    own_sets = [
        pltpu.make_async_copy(
            result.at[which, 2 * (served - 1) + core], column_block(out_ref, owner), own_sems.at[1 + which]
        )
        for which, owner in enumerate((me, far))
    ]
    for copy in own_sets:
        copy.start()

    wait_for(slab.at[pl.ds(0, n_member - 1)], send_sems.at[0])
    wait_for(part.at[pl.ds(0, n_all - 1)], send_sems.at[1])
    wait_for(dist.at[pl.ds(0, n_all - 1)], send_sems.at[2])
    wait_for(twin.at[pl.ds(0, n_member - 1)], send_sems.at[4])
    for copy in own_sets:
        copy.wait()
    wait_for(out_ref.at[:, pl.ds(0, (n_member - 2) * cols)], send_sems.at[3])
    wait_for(out_ref.at[:, pl.ds(0, (n_member - 2) * cols)], recv_sems.at[3])


def per_device(n_member, n_state, ensemble, obs_count):
    rows, width = ensemble.shape
    members, cols = rows * n_member, width // n_member
    half, n_all = members // 2, n_member * n_state
    return pl.pallas_call(
        functools.partial(kernel, n_member, n_state, width * n_state),
        out_shape=jax.ShapeDtypeStruct((rows, width), jnp.bfloat16),
        in_specs=[pl.BlockSpec(memory_space=pl.ANY), pl.BlockSpec(memory_space=pl.ANY)],
        out_specs=pl.BlockSpec(memory_space=pl.ANY),
        scratch_shapes=[
            pltpu.VMEM((rows, width), jnp.bfloat16),
            pltpu.VMEM((n_member, rows, cols), jnp.bfloat16),
            pltpu.VMEM((n_member, rows, cols), jnp.bfloat16),
            pltpu.VMEM((1, members), jnp.int32),
            pltpu.VMEM((n_all, 2, half), jnp.float32),
            pltpu.VMEM((n_all, 2, half), jnp.float32),
            pltpu.VMEM((n_all, 2, half), jnp.float32),
            pltpu.VMEM((members, members), jnp.float32),
            pltpu.VMEM((n_member // 2, 2 * rows, members), jnp.bfloat16),
            pltpu.VMEM((2, n_member // 2, rows, cols), jnp.bfloat16),
            pltpu.SemaphoreType.DMA((4,)),
            pltpu.SemaphoreType.DMA((5,)),
            pltpu.SemaphoreType.DMA((5,)),
            pltpu.SemaphoreType.REGULAR,
        ],
        compiler_params=pltpu.CompilerParams(
            collective_id=0, has_side_effects=True, vmem_limit_bytes=53 * 1024 * 1024
        ),
    )(
        pltpu.with_memory_space_constraint(ensemble, pltpu.HBM),
        pltpu.with_memory_space_constraint(obs_count.reshape(1, members), pltpu.HBM),
    )


def solution(mesh):
    body = functools.partial(per_device, mesh.shape["member"], mesh.shape["state"])
    return jax.shard_map(
        body, mesh=mesh, in_specs=(P("member", "state"), P()), out_specs=P("member", "state"),
        check_vma=False,
    )
```

```python
import functools
import math

import jax
import jax.numpy as jnp
from jax import lax
from jax.experimental import pallas as pl
from jax.experimental.pallas import tpu as pltpu
from jax.sharding import PartitionSpec as P

SWEEPS = 20
LIFT = 80.0
MESH = pl.DeviceIdType.MESH
LOG2E = math.log2(math.e)


def nearness(offset):
    steps = [min(step, 4 - step) for step in offset[:3]]
    return (-sum(steps), max(steps), offset[3])


OFFSETS = sorted(
    (
        (x, z, y, c)
        for x in range(4) for z in range(4) for y in range(4) for c in range(2)
        if (x, z, y, c) != (0, 0, 0, 0)
    ),
    key=nearness,
)


NEAR = (
    ((2, 0), (1, 1), (1, 3), (1, 0), (3, 0), (0, 1), (0, 3), (0, 0)),
    ((0, 2), (3, 3), (3, 1), (1, 0), (3, 0), (0, 1), (0, 3), (0, 0)),
)
FAR_CHIPS = 3


def near_chips():
    me = lax.axis_index("member")
    z, y, c = lax.div(me, 8), lax.rem(lax.div(me, 2), 4), lax.rem(me, 2)
    return [
        lax.rem(z + a[0] + c * (b[0] - a[0]) + 4, 4) * 4 + lax.rem(y + a[1] + c * (b[1] - a[1]) + 4, 4)
        for a, b in zip(*NEAR)
    ]


def antipode(member):
    z, y, c = lax.div(member, 8), lax.rem(lax.div(member, 2), 4), lax.rem(member, 2)
    return lax.rem(z + 2, 4) * 8 + lax.rem(y + 2, 4) * 2 + c


def others():
    plane, me = lax.axis_index("state"), lax.axis_index("member")
    z, y, c = lax.div(me, 8), lax.rem(lax.div(me, 2), 4), lax.rem(me, 2)
    planes = [lax.rem(plane + step, 4) for step in range(4)]
    layers = [lax.rem(z + step, 4) * 8 for step in range(4)]
    lines = [lax.rem(y + step, 4) * 2 for step in range(4)]
    cores = [c, 1 - c]
    members = {
        (dz, dy, dc): layers[dz] + lines[dy] + cores[dc]
        for dz in range(4) for dy in range(4) for dc in range(2)
    }
    everyone = [(planes[dx], members[dz, dy, dc]) for dx, dz, dy, dc in OFFSETS]
    peers = [members[dz, dy, dc] for dx, dz, dy, dc in OFFSETS if dx == 0]
    return everyone, peers


def kernel(
    n_member, n_state, total,
    ens_ref, obs_ref, out_ref,
    own, slab, twin, obs, part, part_in, dist, cost_ref, plan_ref, result,
    own_sems, send_sems, recv_sems, ready_sem,
):
    rows = ens_ref.shape[0]
    cols = ens_ref.shape[1] // n_member
    members = rows * n_member
    half = members // 2
    me = lax.axis_index("member")
    plane = lax.axis_index("state")
    everyone, peers = others()
    n_all = n_member * n_state
    rank = plane * n_member + me
    planes = [lax.rem(plane + step, n_state) for step in range(1, n_state)]

    barrier = pltpu.get_barrier_semaphore()
    for peer in peers:
        pl.semaphore_signal(barrier, inc=1, device_id={"member": peer}, device_id_type=MESH)
    for other in planes:
        pl.semaphore_signal(barrier, inc=1, device_id={"state": other}, device_id_type=MESH)

    def column_block(ref, index):
        return ref.at[:, pl.ds(pl.multiple_of(index * cols, cols), cols)]

    own_obs = pltpu.make_async_copy(obs_ref, obs, own_sems.at[0])
    own_obs.start()
    staged = pltpu.make_async_copy(ens_ref, own, own_sems.at[3])
    staged.start()
    far = antipode(me)
    own_block = pltpu.make_async_copy(column_block(ens_ref, me), slab.at[me], own_sems.at[1])
    own_block.start()
    own_twin = pltpu.make_async_copy(column_block(ens_ref, far), twin.at[me], own_sems.at[2])
    own_twin.start()
    pl.semaphore_wait(barrier, n_member - 1 + n_state - 1)
    for other in planes:
        pl.semaphore_signal(ready_sem, inc=1, device_id={"state": other}, device_id_type=MESH)

    def send(source, target, phase, device):
        pltpu.make_async_remote_copy(
            src_ref=source,
            dst_ref=target,
            send_sem=send_sems.at[phase],
            recv_sem=recv_sems.at[phase],
            device_id=device,
            device_id_type=MESH,
        ).start()

    def wait_for(ref, sem):
        pltpu.make_async_copy(ref, ref, sem).wait()

    staged.wait()
    for peer in peers:
        send(column_block(own, peer), slab.at[me], 0, {"member": peer})

    own_obs.wait()
    raw = -2.0 * obs[...].astype(jnp.float32)
    logw = (raw - jnp.log(jnp.sum(jnp.exp(raw), axis=1, keepdims=True))) * LOG2E
    row = lax.broadcasted_iota(jnp.int32, (members, members), 0)
    column = lax.broadcasted_iota(jnp.int32, (members, members), 1)
    eye = row == column
    above = row[:half, :half] < column[:half, :half]

    own_block.wait()
    wait_for(slab.at[pl.ds(0, n_member - 1)], recv_sems.at[0])

    held = slab[...].reshape(members, cols)
    gram = lax.dot_general(
        held, held, (((1,), (1,)), ((), ())), preferred_element_type=jnp.float32
    )
    diagonal = jnp.where(eye, gram, 0.0)
    norm_col = jnp.sum(diagonal, axis=1, keepdims=True)
    norm_row = jnp.sum(diagonal, axis=0, keepdims=True)
    apart = norm_col + norm_row - 2.0 * gram
    folded = jnp.where(above, apart[:half, :half], apart[half:, half:])
    part[: n_all // 2] = folded.reshape(n_all // 2, 2, half)
    part[n_all // 2 :] = apart[:half, half:].reshape(n_all // 2, 2, half)

    pl.semaphore_wait(ready_sem, n_state - 1)
    for other, peer in everyone:
        send(
            part.at[other * n_member + peer], part_in.at[rank], 1,
            {"state": other, "member": peer},
        )
    for peer in peers[:8:-1]:
        send(column_block(own, antipode(peer)), twin.at[me], 4, {"member": peer})
    part_in[rank] = part[rank]
    wait_for(part.at[pl.ds(0, n_all - 1)], recv_sems.at[1])
    sums = jnp.sum(part_in[...].reshape(members // 8, 8, half), axis=0)
    dist[rank] = sums[0:2] + sums[2:4] + (sums[4:6] + sums[6:8])
    for other in range(n_state):
        for peer in peers:
            send(dist.at[rank], dist.at[rank], 2, {"state": other, "member": peer})

        @pl.when(plane != other)
        def _():
            send(dist.at[rank], dist.at[rank], 2, {"state": other, "member": me})

    for peer in peers[8::-1]:
        send(column_block(own, antipode(peer)), twin.at[me], 4, {"member": peer})
    wait_for(dist.at[pl.ds(0, n_all - 1)], recv_sems.at[2])

    scale_cost = 16.0 / total * LOG2E
    folded = dist[: n_all // 2].reshape(half, half) * scale_cost
    across = dist[n_all // 2 :].reshape(half, half) * scale_cost
    first = jnp.where(above, folded, 0.0)
    second = folded - first
    cost_ref[:half, :half] = first + first.T
    cost_ref[half:, half:] = second + second.T
    cost_ref[:half, half:] = across
    cost_ref[half:, :half] = across.T
    log_count = math.log2(members)

    weight = jnp.exp2(logw + LIFT)

    def two_sweeps(index, carry):
        f_pot, g_pot = carry
        scaled = jnp.exp2(g_pot + (f_pot + LIFT) - cost_ref[...])
        for again in (True, False):
            sums = jnp.sum(scaled, axis=0, keepdims=True)
            f_pot = f_pot + ((logw + LIFT) - jnp.log2(sums))
            scaled = scaled * (weight / sums)
            sums = jnp.sum(scaled, axis=1, keepdims=True)
            g_pot = g_pot + ((LIFT - log_count) - jnp.log2(sums))
            if again:
                scaled = scaled * (2.0 ** (LIFT - log_count) / sums)
        return (f_pot, g_pot)

    f_pot, g_pot = lax.fori_loop(
        0,
        SWEEPS // 2,
        two_sweeps,
        (jnp.zeros((1, members), jnp.float32), jnp.zeros((members, 1), jnp.float32)),
        unroll=5,
    )
    plan = jnp.exp2(g_pot + f_pot - cost_ref[...] + log_count).astype(jnp.bfloat16)
    n_chips = n_member // 2
    plan_ref[...] = plan.reshape(n_chips, 2 * rows, members)
    own_twin.wait()
    wait_for(twin.at[pl.ds(0, n_member - 1)], recv_sems.at[4])

    chips = near_chips()
    served = len(chips)
    core = lax.rem(me, 2)
    mine = jnp.concatenate([plan_ref[chip] for chip in chips], axis=0)
    for which, columns in enumerate((slab, twin)):
        analysis = lax.dot_general(
            mine, columns[...].reshape(members, cols), (((1,), (0,)), ((), ())),
            preferred_element_type=jnp.float32,
        )
        result[which] = analysis.reshape(2 * served, rows, cols).astype(jnp.bfloat16)

    def serve(place):
        for which, owner in enumerate((me, far)):
            target = column_block(out_ref, owner)
            if place < served - 1:
                for side in range(2):
                    send(
                        result.at[which, 2 * place + side], target, 3,
                        {"member": chips[place] * 2 + side},
                    )
            else:
                send(
                    result.at[which, 2 * place + 1 - core], target, 3, {"member": me + 1 - 2 * core}
                )

    for turn in range(4):
        for place in range(served):
            pl.when(lax.div(chips[place], 4) == turn)(functools.partial(serve, place))
    own_sets = [
        pltpu.make_async_copy(
            result.at[which, 2 * (served - 1) + core], column_block(out_ref, owner), own_sems.at[1 + which]
        )
        for which, owner in enumerate((me, far))
    ]
    for copy in own_sets:
        copy.start()

    wait_for(slab.at[pl.ds(0, n_member - 1)], send_sems.at[0])
    wait_for(part.at[pl.ds(0, n_all - 1)], send_sems.at[1])
    wait_for(dist.at[pl.ds(0, n_all - 1)], send_sems.at[2])
    wait_for(twin.at[pl.ds(0, n_member - 1)], send_sems.at[4])
    for copy in own_sets:
        copy.wait()
    wait_for(out_ref.at[:, pl.ds(0, (n_member - 2) * cols)], send_sems.at[3])
    wait_for(out_ref.at[:, pl.ds(0, (n_member - 2) * cols)], recv_sems.at[3])


def per_device(n_member, n_state, ensemble, obs_count):
    rows, width = ensemble.shape
    members, cols = rows * n_member, width // n_member
    half, n_all = members // 2, n_member * n_state
    return pl.pallas_call(
        functools.partial(kernel, n_member, n_state, width * n_state),
        out_shape=jax.ShapeDtypeStruct((rows, width), jnp.bfloat16),
        in_specs=[pl.BlockSpec(memory_space=pl.ANY), pl.BlockSpec(memory_space=pl.ANY)],
        out_specs=pl.BlockSpec(memory_space=pl.ANY),
        scratch_shapes=[
            pltpu.VMEM((rows, width), jnp.bfloat16),
            pltpu.VMEM((n_member, rows, cols), jnp.bfloat16),
            pltpu.VMEM((n_member, rows, cols), jnp.bfloat16),
            pltpu.VMEM((1, members), jnp.int32),
            pltpu.VMEM((n_all, 2, half), jnp.float32),
            pltpu.VMEM((n_all, 2, half), jnp.float32),
            pltpu.VMEM((n_all, 2, half), jnp.float32),
            pltpu.VMEM((members, members), jnp.float32),
            pltpu.VMEM((n_member // 2, 2 * rows, members), jnp.bfloat16),
            pltpu.VMEM((2, n_member // 2, rows, cols), jnp.bfloat16),
            pltpu.SemaphoreType.DMA((4,)),
            pltpu.SemaphoreType.DMA((5,)),
            pltpu.SemaphoreType.DMA((5,)),
            pltpu.SemaphoreType.REGULAR,
        ],
        compiler_params=pltpu.CompilerParams(
            collective_id=0, has_side_effects=True, vmem_limit_bytes=53 * 1024 * 1024
        ),
    )(
        pltpu.with_memory_space_constraint(ensemble, pltpu.HBM),
        pltpu.with_memory_space_constraint(obs_count.reshape(1, members), pltpu.HBM),
    )


def solution(mesh):
    body = functools.partial(per_device, mesh.shape["member"], mesh.shape["state"])
    return jax.shard_map(
        body, mesh=mesh, in_specs=(P("member", "state"), P()), out_specs=P("member", "state"),
        check_vma=False,
    )
```

```python
import functools
import math

import jax
import jax.numpy as jnp
from jax import lax
from jax.experimental import pallas as pl
from jax.experimental.pallas import tpu as pltpu
from jax.sharding import PartitionSpec as P

SWEEPS = 20
LIFT = 80.0
MESH = pl.DeviceIdType.MESH
LOG2E = math.log2(math.e)


def nearness(offset):
    steps = [min(step, 4 - step) for step in offset[:3]]
    return (-sum(steps), max(steps), offset[3])


OFFSETS = sorted(
    (
        (x, z, y, c)
        for x in range(4) for z in range(4) for y in range(4) for c in range(2)
        if (x, z, y, c) != (0, 0, 0, 0)
    ),
    key=nearness,
)


NEAR = (
    ((2, 0), (1, 1), (1, 3), (1, 0), (3, 0), (0, 1), (0, 3), (0, 0)),
    ((0, 2), (3, 3), (3, 1), (1, 0), (3, 0), (0, 1), (0, 3), (0, 0)),
)
FAR_CHIPS = 3


def near_chips():
    me = lax.axis_index("member")
    z, y, c = lax.div(me, 8), lax.rem(lax.div(me, 2), 4), lax.rem(me, 2)
    return [
        lax.rem(z + a[0] + c * (b[0] - a[0]) + 4, 4) * 4 + lax.rem(y + a[1] + c * (b[1] - a[1]) + 4, 4)
        for a, b in zip(*NEAR)
    ]


def antipode(member):
    z, y, c = lax.div(member, 8), lax.rem(lax.div(member, 2), 4), lax.rem(member, 2)
    return lax.rem(z + 2, 4) * 8 + lax.rem(y + 2, 4) * 2 + c


def others():
    plane, me = lax.axis_index("state"), lax.axis_index("member")
    z, y, c = lax.div(me, 8), lax.rem(lax.div(me, 2), 4), lax.rem(me, 2)
    planes = [lax.rem(plane + step, 4) for step in range(4)]
    layers = [lax.rem(z + step, 4) * 8 for step in range(4)]
    lines = [lax.rem(y + step, 4) * 2 for step in range(4)]
    cores = [c, 1 - c]
    members = {
        (dz, dy, dc): layers[dz] + lines[dy] + cores[dc]
        for dz in range(4) for dy in range(4) for dc in range(2)
    }
    everyone = [(planes[dx], members[dz, dy, dc]) for dx, dz, dy, dc in OFFSETS]
    peers = [members[dz, dy, dc] for dx, dz, dy, dc in OFFSETS if dx == 0]
    return everyone, peers


def kernel(
    n_member, n_state, total,
    ens_ref, obs_ref, out_ref,
    own, slab, twin, obs, part, part_in, dist, cost_ref, plan_ref, result,
    own_sems, send_sems, recv_sems, ready_sem,
):
    rows = ens_ref.shape[0]
    cols = ens_ref.shape[1] // n_member
    members = rows * n_member
    half = members // 2
    me = lax.axis_index("member")
    plane = lax.axis_index("state")
    everyone, peers = others()
    n_all = n_member * n_state
    rank = plane * n_member + me
    planes = [lax.rem(plane + step, n_state) for step in range(1, n_state)]

    barrier = pltpu.get_barrier_semaphore()
    for peer in peers:
        pl.semaphore_signal(barrier, inc=1, device_id={"member": peer}, device_id_type=MESH)
    for other in planes:
        pl.semaphore_signal(barrier, inc=1, device_id={"state": other}, device_id_type=MESH)

    def column_block(ref, index):
        return ref.at[:, pl.ds(pl.multiple_of(index * cols, cols), cols)]

    own_obs = pltpu.make_async_copy(obs_ref, obs, own_sems.at[0])
    own_obs.start()
    staged = pltpu.make_async_copy(ens_ref, own, own_sems.at[3])
    staged.start()
    far = antipode(me)
    own_block = pltpu.make_async_copy(column_block(ens_ref, me), slab.at[me], own_sems.at[1])
    own_block.start()
    own_twin = pltpu.make_async_copy(column_block(ens_ref, far), twin.at[me], own_sems.at[2])
    own_twin.start()
    pl.semaphore_wait(barrier, n_member - 1 + n_state - 1)
    for other in planes:
        pl.semaphore_signal(ready_sem, inc=1, device_id={"state": other}, device_id_type=MESH)

    def send(source, target, phase, device):
        pltpu.make_async_remote_copy(
            src_ref=source,
            dst_ref=target,
            send_sem=send_sems.at[phase],
            recv_sem=recv_sems.at[phase],
            device_id=device,
            device_id_type=MESH,
        ).start()

    def wait_for(ref, sem):
        pltpu.make_async_copy(ref, ref, sem).wait()

    staged.wait()
    for peer in peers:
        send(column_block(own, peer), slab.at[me], 0, {"member": peer})

    own_obs.wait()
    raw = -2.0 * obs[...].astype(jnp.float32)
    logw = (raw - jnp.log(jnp.sum(jnp.exp(raw), axis=1, keepdims=True))) * LOG2E
    row = lax.broadcasted_iota(jnp.int32, (members, members), 0)
    column = lax.broadcasted_iota(jnp.int32, (members, members), 1)
    eye = row == column
    above = row[:half, :half] < column[:half, :half]

    own_block.wait()
    wait_for(slab.at[pl.ds(0, n_member - 1)], recv_sems.at[0])

    held = slab[...].reshape(members, cols)
    gram = lax.dot_general(
        held, held, (((1,), (1,)), ((), ())), preferred_element_type=jnp.float32
    )
    diagonal = jnp.where(eye, gram, 0.0)
    norm_col = jnp.sum(diagonal, axis=1, keepdims=True)
    norm_row = jnp.sum(diagonal, axis=0, keepdims=True)
    apart = norm_col + norm_row - 2.0 * gram
    folded = jnp.where(above, apart[:half, :half], apart[half:, half:])
    part[: n_all // 2] = folded.reshape(n_all // 2, 2, half)
    part[n_all // 2 :] = apart[:half, half:].reshape(n_all // 2, 2, half)

    pl.semaphore_wait(ready_sem, n_state - 1)
    for other, peer in everyone:
        send(
            part.at[other * n_member + peer], part_in.at[rank], 1,
            {"state": other, "member": peer},
        )
    for peer in peers[:8:-1]:
        send(column_block(own, antipode(peer)), twin.at[me], 4, {"member": peer})
    part_in[rank] = part[rank]
    wait_for(part.at[pl.ds(0, n_all - 1)], recv_sems.at[1])
    sums = jnp.sum(part_in[...].reshape(members // 8, 8, half), axis=0)
    dist[rank] = sums[0:2] + sums[2:4] + (sums[4:6] + sums[6:8])
    for other in range(n_state):
        for peer in peers:
            send(dist.at[rank], dist.at[rank], 2, {"state": other, "member": peer})

        @pl.when(plane != other)
        def _():
            send(dist.at[rank], dist.at[rank], 2, {"state": other, "member": me})

    for peer in peers[8::-1]:
        send(column_block(own, antipode(peer)), twin.at[me], 4, {"member": peer})
    wait_for(dist.at[pl.ds(0, n_all - 1)], recv_sems.at[2])

    scale_cost = 16.0 / total * LOG2E
    folded = dist[: n_all // 2].reshape(half, half) * scale_cost
    across = dist[n_all // 2 :].reshape(half, half) * scale_cost
    first = jnp.where(above, folded, 0.0)
    second = folded - first
    cost_ref[:half, :half] = first + first.T
    cost_ref[half:, half:] = second + second.T
    cost_ref[:half, half:] = across
    cost_ref[half:, :half] = across.T
    log_count = math.log2(members)

    weight = jnp.exp2(logw + LIFT)

    def two_sweeps(index, carry):
        f_pot, g_pot = carry
        scaled = jnp.exp2(g_pot + (f_pot + LIFT) - cost_ref[...])
        for again in (True, False):
            sums = jnp.sum(scaled, axis=0, keepdims=True)
            f_pot = f_pot + ((logw + LIFT) - jnp.log2(sums))
            scaled = scaled * (weight / sums)
            sums = jnp.sum(scaled, axis=1, keepdims=True)
            g_pot = g_pot + ((LIFT - log_count) - jnp.log2(sums))
            if again:
                scaled = scaled * (2.0 ** (LIFT - log_count) / sums)
        return (f_pot, g_pot)

    f_pot, g_pot = lax.fori_loop(
        0,
        SWEEPS // 2 - 1,
        two_sweeps,
        (jnp.zeros((1, members), jnp.float32), jnp.zeros((members, 1), jnp.float32)),
        unroll=3,
    )
    scaled = jnp.exp2(g_pot + (f_pot + LIFT) - cost_ref[...])
    scaled = scaled * (weight / jnp.sum(scaled, axis=0, keepdims=True))
    scaled = scaled * (2.0 ** (LIFT - log_count) / jnp.sum(scaled, axis=1, keepdims=True))
    scaled = scaled * (weight / jnp.sum(scaled, axis=0, keepdims=True))
    plan = (scaled * (1.0 / jnp.sum(scaled, axis=1, keepdims=True))).astype(jnp.bfloat16)
    n_chips = n_member // 2
    plan_ref[...] = plan.reshape(n_chips, 2 * rows, members)
    own_twin.wait()
    wait_for(twin.at[pl.ds(0, n_member - 1)], recv_sems.at[4])

    chips = near_chips()
    served = len(chips)
    core = lax.rem(me, 2)
    mine = jnp.concatenate([plan_ref[chip] for chip in chips], axis=0)
    for which, columns in enumerate((slab, twin)):
        analysis = lax.dot_general(
            mine, columns[...].reshape(members, cols), (((1,), (0,)), ((), ())),
            preferred_element_type=jnp.float32,
        )
        result[which] = analysis.reshape(2 * served, rows, cols).astype(jnp.bfloat16)

    def serve(place):
        for which, owner in enumerate((me, far)):
            target = column_block(out_ref, owner)
            if place < served - 1:
                for side in range(2):
                    send(
                        result.at[which, 2 * place + side], target, 3,
                        {"member": chips[place] * 2 + side},
                    )
            else:
                send(
                    result.at[which, 2 * place + 1 - core], target, 3, {"member": me + 1 - 2 * core}
                )

    for turn in range(4):
        for place in range(served):
            pl.when(lax.div(chips[place], 4) == turn)(functools.partial(serve, place))
    own_sets = [
        pltpu.make_async_copy(
            result.at[which, 2 * (served - 1) + core], column_block(out_ref, owner), own_sems.at[1 + which]
        )
        for which, owner in enumerate((me, far))
    ]
    for copy in own_sets:
        copy.start()

    wait_for(slab.at[pl.ds(0, n_member - 1)], send_sems.at[0])
    wait_for(part.at[pl.ds(0, n_all - 1)], send_sems.at[1])
    wait_for(dist.at[pl.ds(0, n_all - 1)], send_sems.at[2])
    wait_for(twin.at[pl.ds(0, n_member - 1)], send_sems.at[4])
    for copy in own_sets:
        copy.wait()
    wait_for(out_ref.at[:, pl.ds(0, (n_member - 2) * cols)], send_sems.at[3])
    wait_for(out_ref.at[:, pl.ds(0, (n_member - 2) * cols)], recv_sems.at[3])


def per_device(n_member, n_state, ensemble, obs_count):
    rows, width = ensemble.shape
    members, cols = rows * n_member, width // n_member
    half, n_all = members // 2, n_member * n_state
    return pl.pallas_call(
        functools.partial(kernel, n_member, n_state, width * n_state),
        out_shape=jax.ShapeDtypeStruct((rows, width), jnp.bfloat16),
        in_specs=[pl.BlockSpec(memory_space=pl.ANY), pl.BlockSpec(memory_space=pl.ANY)],
        out_specs=pl.BlockSpec(memory_space=pl.ANY),
        scratch_shapes=[
            pltpu.VMEM((rows, width), jnp.bfloat16),
            pltpu.VMEM((n_member, rows, cols), jnp.bfloat16),
            pltpu.VMEM((n_member, rows, cols), jnp.bfloat16),
            pltpu.VMEM((1, members), jnp.int32),
            pltpu.VMEM((n_all, 2, half), jnp.float32),
            pltpu.VMEM((n_all, 2, half), jnp.float32),
            pltpu.VMEM((n_all, 2, half), jnp.float32),
            pltpu.VMEM((members, members), jnp.float32),
            pltpu.VMEM((n_member // 2, 2 * rows, members), jnp.bfloat16),
            pltpu.VMEM((2, n_member // 2, rows, cols), jnp.bfloat16),
            pltpu.SemaphoreType.DMA((4,)),
            pltpu.SemaphoreType.DMA((5,)),
            pltpu.SemaphoreType.DMA((5,)),
            pltpu.SemaphoreType.REGULAR,
        ],
        compiler_params=pltpu.CompilerParams(
            collective_id=0, has_side_effects=True, vmem_limit_bytes=53 * 1024 * 1024
        ),
    )(
        pltpu.with_memory_space_constraint(ensemble, pltpu.HBM),
        pltpu.with_memory_space_constraint(obs_count.reshape(1, members), pltpu.HBM),
    )


def solution(mesh):
    body = functools.partial(per_device, mesh.shape["member"], mesh.shape["state"])
    return jax.shard_map(
        body, mesh=mesh, in_specs=(P("member", "state"), P()), out_specs=P("member", "state"),
        check_vma=False,
    )
```

```python
import functools
import math

import jax
import jax.numpy as jnp
from jax import lax
from jax.experimental import pallas as pl
from jax.experimental.pallas import tpu as pltpu
from jax.sharding import PartitionSpec as P

SWEEPS = 20
LIFT = 80.0
MESH = pl.DeviceIdType.MESH
LOG2E = math.log2(math.e)


def nearness(offset):
    steps = [min(step, 4 - step) for step in offset[:3]]
    return (-sum(steps), max(steps), offset[3])


OFFSETS = sorted(
    (
        (x, z, y, c)
        for x in range(4) for z in range(4) for y in range(4) for c in range(2)
        if (x, z, y, c) != (0, 0, 0, 0)
    ),
    key=nearness,
)


NEAR = (
    ((2, 0), (1, 1), (1, 3), (1, 0), (3, 0), (0, 1), (0, 3), (0, 0)),
    ((0, 2), (3, 3), (3, 1), (1, 0), (3, 0), (0, 1), (0, 3), (0, 0)),
)
FAR_CHIPS = 3


def near_chips():
    me = lax.axis_index("member")
    z, y, c = lax.div(me, 8), lax.rem(lax.div(me, 2), 4), lax.rem(me, 2)
    return [
        lax.rem(z + a[0] + c * (b[0] - a[0]) + 4, 4) * 4 + lax.rem(y + a[1] + c * (b[1] - a[1]) + 4, 4)
        for a, b in zip(*NEAR)
    ]


def antipode(member):
    z, y, c = lax.div(member, 8), lax.rem(lax.div(member, 2), 4), lax.rem(member, 2)
    return lax.rem(z + 2, 4) * 8 + lax.rem(y + 2, 4) * 2 + c


def others():
    plane, me = lax.axis_index("state"), lax.axis_index("member")
    z, y, c = lax.div(me, 8), lax.rem(lax.div(me, 2), 4), lax.rem(me, 2)
    planes = [lax.rem(plane + step, 4) for step in range(4)]
    layers = [lax.rem(z + step, 4) * 8 for step in range(4)]
    lines = [lax.rem(y + step, 4) * 2 for step in range(4)]
    cores = [c, 1 - c]
    members = {
        (dz, dy, dc): layers[dz] + lines[dy] + cores[dc]
        for dz in range(4) for dy in range(4) for dc in range(2)
    }
    everyone = [(planes[dx], members[dz, dy, dc]) for dx, dz, dy, dc in OFFSETS]
    peers = [members[dz, dy, dc] for dx, dz, dy, dc in OFFSETS if dx == 0]
    return everyone, peers


def kernel(
    n_member, n_state, total,
    ens_ref, obs_ref, out_ref,
    own, slab, twin, obs, part, part_in, dist, cost_ref, plan_ref, result,
    own_sems, send_sems, recv_sems, ready_sem,
):
    rows = ens_ref.shape[0]
    cols = ens_ref.shape[1] // n_member
    members = rows * n_member
    half = members // 2
    me = lax.axis_index("member")
    plane = lax.axis_index("state")
    everyone, peers = others()
    n_all = n_member * n_state
    rank = plane * n_member + me
    planes = [lax.rem(plane + step, n_state) for step in range(1, n_state)]

    barrier = pltpu.get_barrier_semaphore()
    for peer in peers:
        pl.semaphore_signal(barrier, inc=1, device_id={"member": peer}, device_id_type=MESH)
    for other in planes:
        pl.semaphore_signal(barrier, inc=1, device_id={"state": other}, device_id_type=MESH)

    def column_block(ref, index):
        return ref.at[:, pl.ds(pl.multiple_of(index * cols, cols), cols)]

    own_obs = pltpu.make_async_copy(obs_ref, obs, own_sems.at[0])
    own_obs.start()
    staged = pltpu.make_async_copy(ens_ref, own, own_sems.at[3])
    staged.start()
    far = antipode(me)
    own_block = pltpu.make_async_copy(column_block(ens_ref, me), slab.at[me], own_sems.at[1])
    own_block.start()
    own_twin = pltpu.make_async_copy(column_block(ens_ref, far), twin.at[me], own_sems.at[2])
    own_twin.start()
    pl.semaphore_wait(barrier, n_member - 1 + n_state - 1)
    for other in planes:
        pl.semaphore_signal(ready_sem, inc=1, device_id={"state": other}, device_id_type=MESH)

    def send(source, target, phase, device):
        pltpu.make_async_remote_copy(
            src_ref=source,
            dst_ref=target,
            send_sem=send_sems.at[phase],
            recv_sem=recv_sems.at[phase],
            device_id=device,
            device_id_type=MESH,
        ).start()

    def wait_for(ref, sem):
        pltpu.make_async_copy(ref, ref, sem).wait()

    for peer in peers[:12]:
        send(column_block(ens_ref, peer), slab.at[me], 0, {"member": peer})
    staged.wait()
    for peer in peers[12:]:
        send(column_block(own, peer), slab.at[me], 0, {"member": peer})

    own_obs.wait()
    raw = -2.0 * obs[...].astype(jnp.float32)
    logw = (raw - jnp.log(jnp.sum(jnp.exp(raw), axis=1, keepdims=True))) * LOG2E
    row = lax.broadcasted_iota(jnp.int32, (members, members), 0)
    column = lax.broadcasted_iota(jnp.int32, (members, members), 1)
    eye = row == column
    above = row[:half, :half] < column[:half, :half]

    own_block.wait()
    wait_for(slab.at[pl.ds(0, n_member - 1)], recv_sems.at[0])

    held = slab[...].reshape(members, cols)
    gram = lax.dot_general(
        held, held, (((1,), (1,)), ((), ())), preferred_element_type=jnp.float32
    )
    diagonal = jnp.where(eye, gram, 0.0)
    norm_col = jnp.sum(diagonal, axis=1, keepdims=True)
    norm_row = jnp.sum(diagonal, axis=0, keepdims=True)
    apart = norm_col + norm_row - 2.0 * gram
    folded = jnp.where(above, apart[:half, :half], apart[half:, half:])
    part[: n_all // 2] = folded.reshape(n_all // 2, 2, half)
    part[n_all // 2 :] = apart[:half, half:].reshape(n_all // 2, 2, half)

    pl.semaphore_wait(ready_sem, n_state - 1)
    for other, peer in everyone:
        send(
            part.at[other * n_member + peer], part_in.at[rank], 1,
            {"state": other, "member": peer},
        )
    for peer in peers[:8:-1]:
        send(column_block(own, antipode(peer)), twin.at[me], 4, {"member": peer})
    part_in[rank] = part[rank]
    wait_for(part.at[pl.ds(0, n_all - 1)], recv_sems.at[1])
    sums = jnp.sum(part_in[...].reshape(members // 8, 8, half), axis=0)
    dist[rank] = sums[0:2] + sums[2:4] + (sums[4:6] + sums[6:8])
    for other in range(n_state):
        for peer in peers:
            send(dist.at[rank], dist.at[rank], 2, {"state": other, "member": peer})

        @pl.when(plane != other)
        def _():
            send(dist.at[rank], dist.at[rank], 2, {"state": other, "member": me})

    for peer in peers[8::-1]:
        send(column_block(own, antipode(peer)), twin.at[me], 4, {"member": peer})
    wait_for(dist.at[pl.ds(0, n_all - 1)], recv_sems.at[2])

    scale_cost = 16.0 / total * LOG2E
    folded = dist[: n_all // 2].reshape(half, half) * scale_cost
    across = dist[n_all // 2 :].reshape(half, half) * scale_cost
    first = jnp.where(above, folded, 0.0)
    second = folded - first
    cost_ref[:half, :half] = first + first.T
    cost_ref[half:, half:] = second + second.T
    cost_ref[:half, half:] = across
    cost_ref[half:, :half] = across.T
    log_count = math.log2(members)

    weight = jnp.exp2(logw + LIFT)

    def two_sweeps(index, carry):
        f_pot, g_pot = carry
        scaled = jnp.exp2(g_pot + (f_pot + LIFT) - cost_ref[...])
        for again in (True, False):
            sums = jnp.sum(scaled, axis=0, keepdims=True)
            f_pot = f_pot + ((logw + LIFT) - jnp.log2(sums))
            scaled = scaled * (weight / sums)
            sums = jnp.sum(scaled, axis=1, keepdims=True)
            g_pot = g_pot + ((LIFT - log_count) - jnp.log2(sums))
            if again:
                scaled = scaled * (2.0 ** (LIFT - log_count) / sums)
        return (f_pot, g_pot)

    f_pot, g_pot = lax.fori_loop(
        0,
        SWEEPS // 2 - 1,
        two_sweeps,
        (jnp.zeros((1, members), jnp.float32), jnp.zeros((members, 1), jnp.float32)),
        unroll=3,
    )
    scaled = jnp.exp2(g_pot + (f_pot + LIFT) - cost_ref[...])
    scaled = scaled * (weight / jnp.sum(scaled, axis=0, keepdims=True))
    scaled = scaled * (2.0 ** (LIFT - log_count) / jnp.sum(scaled, axis=1, keepdims=True))
    scaled = scaled * (weight / jnp.sum(scaled, axis=0, keepdims=True))
    plan = (scaled * (1.0 / jnp.sum(scaled, axis=1, keepdims=True))).astype(jnp.bfloat16)
    n_chips = n_member // 2
    plan_ref[...] = plan.reshape(n_chips, 2 * rows, members)
    own_twin.wait()
    wait_for(twin.at[pl.ds(0, n_member - 1)], recv_sems.at[4])

    chips = near_chips()
    served = len(chips)
    core = lax.rem(me, 2)
    mine = jnp.concatenate([plan_ref[chip] for chip in chips], axis=0)
    for which, columns in enumerate((slab, twin)):
        analysis = lax.dot_general(
            mine, columns[...].reshape(members, cols), (((1,), (0,)), ((), ())),
            preferred_element_type=jnp.float32,
        )
        result[which] = analysis.reshape(2 * served, rows, cols).astype(jnp.bfloat16)

    def serve(place):
        for which, owner in enumerate((me, far)):
            target = column_block(out_ref, owner)
            if place < served - 1:
                for side in range(2):
                    send(
                        result.at[which, 2 * place + side], target, 3,
                        {"member": chips[place] * 2 + side},
                    )
            else:
                send(
                    result.at[which, 2 * place + 1 - core], target, 3, {"member": me + 1 - 2 * core}
                )

    for turn in range(4):
        for place in range(served):
            pl.when(lax.div(chips[place], 4) == turn)(functools.partial(serve, place))
    own_sets = [
        pltpu.make_async_copy(
            result.at[which, 2 * (served - 1) + core], column_block(out_ref, owner), own_sems.at[1 + which]
        )
        for which, owner in enumerate((me, far))
    ]
    for copy in own_sets:
        copy.start()

    wait_for(slab.at[pl.ds(0, n_member - 1)], send_sems.at[0])
    wait_for(part.at[pl.ds(0, n_all - 1)], send_sems.at[1])
    wait_for(dist.at[pl.ds(0, n_all - 1)], send_sems.at[2])
    wait_for(twin.at[pl.ds(0, n_member - 1)], send_sems.at[4])
    for copy in own_sets:
        copy.wait()
    wait_for(out_ref.at[:, pl.ds(0, (n_member - 2) * cols)], send_sems.at[3])
    wait_for(out_ref.at[:, pl.ds(0, (n_member - 2) * cols)], recv_sems.at[3])


def per_device(n_member, n_state, ensemble, obs_count):
    rows, width = ensemble.shape
    members, cols = rows * n_member, width // n_member
    half, n_all = members // 2, n_member * n_state
    return pl.pallas_call(
        functools.partial(kernel, n_member, n_state, width * n_state),
        out_shape=jax.ShapeDtypeStruct((rows, width), jnp.bfloat16),
        in_specs=[pl.BlockSpec(memory_space=pl.ANY), pl.BlockSpec(memory_space=pl.ANY)],
        out_specs=pl.BlockSpec(memory_space=pl.ANY),
        scratch_shapes=[
            pltpu.VMEM((rows, width), jnp.bfloat16),
            pltpu.VMEM((n_member, rows, cols), jnp.bfloat16),
            pltpu.VMEM((n_member, rows, cols), jnp.bfloat16),
            pltpu.VMEM((1, members), jnp.int32),
            pltpu.VMEM((n_all, 2, half), jnp.float32),
            pltpu.VMEM((n_all, 2, half), jnp.float32),
            pltpu.VMEM((n_all, 2, half), jnp.float32),
            pltpu.VMEM((members, members), jnp.float32),
            pltpu.VMEM((n_member // 2, 2 * rows, members), jnp.bfloat16),
            pltpu.VMEM((2, n_member // 2, rows, cols), jnp.bfloat16),
            pltpu.SemaphoreType.DMA((4,)),
            pltpu.SemaphoreType.DMA((5,)),
            pltpu.SemaphoreType.DMA((5,)),
            pltpu.SemaphoreType.REGULAR,
        ],
        compiler_params=pltpu.CompilerParams(
            collective_id=0, has_side_effects=True, vmem_limit_bytes=53 * 1024 * 1024
        ),
    )(
        pltpu.with_memory_space_constraint(ensemble, pltpu.HBM),
        pltpu.with_memory_space_constraint(obs_count.reshape(1, members), pltpu.HBM),
    )


def solution(mesh):
    body = functools.partial(per_device, mesh.shape["member"], mesh.shape["state"])
    return jax.shard_map(
        body, mesh=mesh, in_specs=(P("member", "state"), P()), out_specs=P("member", "state"),
        check_vma=False,
    )
```

```python
import functools
import math

import jax
import jax.numpy as jnp
from jax import lax
from jax.experimental import pallas as pl
from jax.experimental.pallas import tpu as pltpu
from jax.sharding import PartitionSpec as P

SWEEPS = 20
LIFT = 80.0
MESH = pl.DeviceIdType.MESH
LOG2E = math.log2(math.e)


def nearness(offset):
    steps = [min(step, 4 - step) for step in offset[:3]]
    return (-sum(steps), max(steps), offset[3])


OFFSETS = sorted(
    (
        (x, z, y, c)
        for x in range(4) for z in range(4) for y in range(4) for c in range(2)
        if (x, z, y, c) != (0, 0, 0, 0)
    ),
    key=nearness,
)


NEAR = (
    ((2, 0), (1, 1), (1, 3), (1, 0), (3, 0), (0, 1), (0, 3), (0, 0)),
    ((0, 2), (3, 3), (3, 1), (1, 0), (3, 0), (0, 1), (0, 3), (0, 0)),
)
FAR_CHIPS = 3


def near_chips():
    me = lax.axis_index("member")
    z, y, c = lax.div(me, 8), lax.rem(lax.div(me, 2), 4), lax.rem(me, 2)
    return [
        lax.rem(z + a[0] + c * (b[0] - a[0]) + 4, 4) * 4 + lax.rem(y + a[1] + c * (b[1] - a[1]) + 4, 4)
        for a, b in zip(*NEAR)
    ]


def antipode(member):
    z, y, c = lax.div(member, 8), lax.rem(lax.div(member, 2), 4), lax.rem(member, 2)
    return lax.rem(z + 2, 4) * 8 + lax.rem(y + 2, 4) * 2 + c


def others():
    plane, me = lax.axis_index("state"), lax.axis_index("member")
    z, y, c = lax.div(me, 8), lax.rem(lax.div(me, 2), 4), lax.rem(me, 2)
    planes = [lax.rem(plane + step, 4) for step in range(4)]
    layers = [lax.rem(z + step, 4) * 8 for step in range(4)]
    lines = [lax.rem(y + step, 4) * 2 for step in range(4)]
    cores = [c, 1 - c]
    members = {
        (dz, dy, dc): layers[dz] + lines[dy] + cores[dc]
        for dz in range(4) for dy in range(4) for dc in range(2)
    }
    everyone = [(planes[dx], members[dz, dy, dc]) for dx, dz, dy, dc in OFFSETS]
    peers = [members[dz, dy, dc] for dx, dz, dy, dc in OFFSETS if dx == 0]
    return everyone, peers


def kernel(
    n_member, n_state, total,
    ens_ref, obs_ref, out_ref,
    own, slab, twin, obs, part, part_in, dist, cost_ref, plan_ref, result,
    own_sems, send_sems, recv_sems, ready_sem,
):
    rows = ens_ref.shape[0]
    cols = ens_ref.shape[1] // n_member
    members = rows * n_member
    half = members // 2
    me = lax.axis_index("member")
    plane = lax.axis_index("state")
    everyone, peers = others()
    n_all = n_member * n_state
    rank = plane * n_member + me
    planes = [lax.rem(plane + step, n_state) for step in range(1, n_state)]

    barrier = pltpu.get_barrier_semaphore()
    for peer in peers:
        pl.semaphore_signal(barrier, inc=1, device_id={"member": peer}, device_id_type=MESH)
    for other in planes:
        pl.semaphore_signal(barrier, inc=1, device_id={"state": other}, device_id_type=MESH)

    def column_block(ref, index):
        return ref.at[:, pl.ds(pl.multiple_of(index * cols, cols), cols)]

    own_obs = pltpu.make_async_copy(obs_ref, obs, own_sems.at[0])
    own_obs.start()
    staged = pltpu.make_async_copy(ens_ref, own, own_sems.at[3])
    staged.start()
    far = antipode(me)
    own_block = pltpu.make_async_copy(column_block(ens_ref, me), slab.at[me], own_sems.at[1])
    own_block.start()
    own_twin = pltpu.make_async_copy(column_block(ens_ref, far), twin.at[me], own_sems.at[2])
    pl.semaphore_wait(barrier, n_member - 1 + n_state - 1)
    for other in planes:
        pl.semaphore_signal(ready_sem, inc=1, device_id={"state": other}, device_id_type=MESH)

    def send(source, target, phase, device):
        pltpu.make_async_remote_copy(
            src_ref=source,
            dst_ref=target,
            send_sem=send_sems.at[phase],
            recv_sem=recv_sems.at[phase],
            device_id=device,
            device_id_type=MESH,
        ).start()

    def wait_for(ref, sem):
        pltpu.make_async_copy(ref, ref, sem).wait()

    for peer in peers[:9]:
        send(column_block(ens_ref, peer), slab.at[me], 0, {"member": peer})
    staged.wait()
    for peer in peers[9:]:
        send(column_block(own, peer), slab.at[me], 0, {"member": peer})
    own_twin.start()

    own_obs.wait()
    raw = -2.0 * obs[...].astype(jnp.float32)
    logw = (raw - jnp.log(jnp.sum(jnp.exp(raw), axis=1, keepdims=True))) * LOG2E
    row = lax.broadcasted_iota(jnp.int32, (members, members), 0)
    column = lax.broadcasted_iota(jnp.int32, (members, members), 1)
    eye = row == column
    above = row[:half, :half] < column[:half, :half]

    own_block.wait()
    wait_for(slab.at[pl.ds(0, n_member - 1)], recv_sems.at[0])

    held = slab[...].reshape(members, cols)
    gram = lax.dot_general(
        held, held, (((1,), (1,)), ((), ())), preferred_element_type=jnp.float32
    )
    diagonal = jnp.where(eye, gram, 0.0)
    norm_col = jnp.sum(diagonal, axis=1, keepdims=True)
    norm_row = jnp.sum(diagonal, axis=0, keepdims=True)
    apart = norm_col + norm_row - 2.0 * gram
    folded = jnp.where(above, apart[:half, :half], apart[half:, half:])
    part[: n_all // 2] = folded.reshape(n_all // 2, 2, half)
    part[n_all // 2 :] = apart[:half, half:].reshape(n_all // 2, 2, half)

    pl.semaphore_wait(ready_sem, n_state - 1)
    for other, peer in everyone:
        send(
            part.at[other * n_member + peer], part_in.at[rank], 1,
            {"state": other, "member": peer},
        )
    for peer in peers[:8:-1]:
        send(column_block(own, antipode(peer)), twin.at[me], 4, {"member": peer})
    part_in[rank] = part[rank]
    wait_for(part.at[pl.ds(0, n_all - 1)], recv_sems.at[1])
    sums = jnp.sum(part_in[...].reshape(members // 8, 8, half), axis=0)
    dist[rank] = sums[0:2] + sums[2:4] + (sums[4:6] + sums[6:8])
    for other in range(n_state):
        for peer in peers:
            send(dist.at[rank], dist.at[rank], 2, {"state": other, "member": peer})

        @pl.when(plane != other)
        def _():
            send(dist.at[rank], dist.at[rank], 2, {"state": other, "member": me})

    for peer in peers[8::-1]:
        send(column_block(own, antipode(peer)), twin.at[me], 4, {"member": peer})
    wait_for(dist.at[pl.ds(0, n_all - 1)], recv_sems.at[2])

    scale_cost = 16.0 / total * LOG2E
    folded = dist[: n_all // 2].reshape(half, half) * scale_cost
    across = dist[n_all // 2 :].reshape(half, half) * scale_cost
    first = jnp.where(above, folded, 0.0)
    second = folded - first
    cost_ref[:half, :half] = first + first.T
    cost_ref[half:, half:] = second + second.T
    cost_ref[:half, half:] = across
    cost_ref[half:, :half] = across.T
    log_count = math.log2(members)

    weight = jnp.exp2(logw + LIFT)

    def two_sweeps(index, carry):
        f_pot, g_pot = carry
        scaled = jnp.exp2(g_pot + (f_pot + LIFT) - cost_ref[...])
        for again in (True, False):
            sums = jnp.sum(scaled, axis=0, keepdims=True)
            f_pot = f_pot + ((logw + LIFT) - jnp.log2(sums))
            scaled = scaled * (weight / sums)
            sums = jnp.sum(scaled, axis=1, keepdims=True)
            g_pot = g_pot + ((LIFT - log_count) - jnp.log2(sums))
            if again:
                scaled = scaled * (2.0 ** (LIFT - log_count) / sums)
        return (f_pot, g_pot)

    f_pot, g_pot = lax.fori_loop(
        0,
        SWEEPS // 2 - 1,
        two_sweeps,
        (jnp.zeros((1, members), jnp.float32), jnp.zeros((members, 1), jnp.float32)),
        unroll=3,
    )
    scaled = jnp.exp2(g_pot + (f_pot + LIFT) - cost_ref[...])
    scaled = scaled * (weight / jnp.sum(scaled, axis=0, keepdims=True))
    scaled = scaled * (2.0 ** (LIFT - log_count) / jnp.sum(scaled, axis=1, keepdims=True))
    scaled = scaled * (weight / jnp.sum(scaled, axis=0, keepdims=True))
    plan = (scaled * (1.0 / jnp.sum(scaled, axis=1, keepdims=True))).astype(jnp.bfloat16)
    n_chips = n_member // 2
    plan_ref[...] = plan.reshape(n_chips, 2 * rows, members)
    own_twin.wait()
    wait_for(twin.at[pl.ds(0, n_member - 1)], recv_sems.at[4])

    chips = near_chips()
    served = len(chips)
    core = lax.rem(me, 2)
    mine = jnp.concatenate([plan_ref[chip] for chip in chips], axis=0)
    for which, columns in enumerate((slab, twin)):
        analysis = lax.dot_general(
            mine, columns[...].reshape(members, cols), (((1,), (0,)), ((), ())),
            preferred_element_type=jnp.float32,
        )
        result[which] = analysis.reshape(2 * served, rows, cols).astype(jnp.bfloat16)

    def serve(place):
        for which, owner in enumerate((me, far)):
            target = column_block(out_ref, owner)
            if place < served - 1:
                for side in range(2):
                    send(
                        result.at[which, 2 * place + side], target, 3,
                        {"member": chips[place] * 2 + side},
                    )
            else:
                send(
                    result.at[which, 2 * place + 1 - core], target, 3, {"member": me + 1 - 2 * core}
                )

    for turn in range(4):
        for place in range(served):
            pl.when(lax.div(chips[place], 4) == turn)(functools.partial(serve, place))
    own_sets = [
        pltpu.make_async_copy(
            result.at[which, 2 * (served - 1) + core], column_block(out_ref, owner), own_sems.at[1 + which]
        )
        for which, owner in enumerate((me, far))
    ]
    for copy in own_sets:
        copy.start()

    wait_for(slab.at[pl.ds(0, n_member - 1)], send_sems.at[0])
    wait_for(part.at[pl.ds(0, n_all - 1)], send_sems.at[1])
    wait_for(dist.at[pl.ds(0, n_all - 1)], send_sems.at[2])
    wait_for(twin.at[pl.ds(0, n_member - 1)], send_sems.at[4])
    for copy in own_sets:
        copy.wait()
    wait_for(out_ref.at[:, pl.ds(0, (n_member - 2) * cols)], send_sems.at[3])
    wait_for(out_ref.at[:, pl.ds(0, (n_member - 2) * cols)], recv_sems.at[3])


def per_device(n_member, n_state, ensemble, obs_count):
    rows, width = ensemble.shape
    members, cols = rows * n_member, width // n_member
    half, n_all = members // 2, n_member * n_state
    return pl.pallas_call(
        functools.partial(kernel, n_member, n_state, width * n_state),
        out_shape=jax.ShapeDtypeStruct((rows, width), jnp.bfloat16),
        in_specs=[pl.BlockSpec(memory_space=pl.ANY), pl.BlockSpec(memory_space=pl.ANY)],
        out_specs=pl.BlockSpec(memory_space=pl.ANY),
        scratch_shapes=[
            pltpu.VMEM((rows, width), jnp.bfloat16),
            pltpu.VMEM((n_member, rows, cols), jnp.bfloat16),
            pltpu.VMEM((n_member, rows, cols), jnp.bfloat16),
            pltpu.VMEM((1, members), jnp.int32),
            pltpu.VMEM((n_all, 2, half), jnp.float32),
            pltpu.VMEM((n_all, 2, half), jnp.float32),
            pltpu.VMEM((n_all, 2, half), jnp.float32),
            pltpu.VMEM((members, members), jnp.float32),
            pltpu.VMEM((n_member // 2, 2 * rows, members), jnp.bfloat16),
            pltpu.VMEM((2, n_member // 2, rows, cols), jnp.bfloat16),
            pltpu.SemaphoreType.DMA((4,)),
            pltpu.SemaphoreType.DMA((5,)),
            pltpu.SemaphoreType.DMA((5,)),
            pltpu.SemaphoreType.REGULAR,
        ],
        compiler_params=pltpu.CompilerParams(
            collective_id=0, has_side_effects=True, vmem_limit_bytes=53 * 1024 * 1024
        ),
    )(
        pltpu.with_memory_space_constraint(ensemble, pltpu.HBM),
        pltpu.with_memory_space_constraint(obs_count.reshape(1, members), pltpu.HBM),
    )


def solution(mesh):
    body = functools.partial(per_device, mesh.shape["member"], mesh.shape["state"])
    return jax.shard_map(
        body, mesh=mesh, in_specs=(P("member", "state"), P()), out_specs=P("member", "state"),
        check_vma=False,
    )
```

```python
import functools
import math

import jax
import jax.numpy as jnp
from jax import lax
from jax.experimental import pallas as pl
from jax.experimental.pallas import tpu as pltpu
from jax.sharding import PartitionSpec as P

SWEEPS = 20
LIFT = 80.0
MESH = pl.DeviceIdType.MESH
LOG2E = math.log2(math.e)


def nearness(offset):
    steps = [min(step, 4 - step) for step in offset[:3]]
    return (-sum(steps), max(steps), offset[3])


OFFSETS = sorted(
    (
        (x, z, y, c)
        for x in range(4) for z in range(4) for y in range(4) for c in range(2)
        if (x, z, y, c) != (0, 0, 0, 0)
    ),
    key=nearness,
)


NEAR = (
    ((2, 0), (1, 1), (1, 3), (1, 0), (3, 0), (0, 1), (0, 3), (0, 0)),
    ((0, 2), (3, 3), (3, 1), (1, 0), (3, 0), (0, 1), (0, 3), (0, 0)),
)
FAR_CHIPS = 3


def near_chips():
    me = lax.axis_index("member")
    z, y, c = lax.div(me, 8), lax.rem(lax.div(me, 2), 4), lax.rem(me, 2)
    return [
        lax.rem(z + a[0] + c * (b[0] - a[0]) + 4, 4) * 4 + lax.rem(y + a[1] + c * (b[1] - a[1]) + 4, 4)
        for a, b in zip(*NEAR)
    ]


def antipode(member):
    z, y, c = lax.div(member, 8), lax.rem(lax.div(member, 2), 4), lax.rem(member, 2)
    return lax.rem(z + 2, 4) * 8 + lax.rem(y + 2, 4) * 2 + c


def others():
    plane, me = lax.axis_index("state"), lax.axis_index("member")
    z, y, c = lax.div(me, 8), lax.rem(lax.div(me, 2), 4), lax.rem(me, 2)
    planes = [lax.rem(plane + step, 4) for step in range(4)]
    layers = [lax.rem(z + step, 4) * 8 for step in range(4)]
    lines = [lax.rem(y + step, 4) * 2 for step in range(4)]
    cores = [c, 1 - c]
    members = {
        (dz, dy, dc): layers[dz] + lines[dy] + cores[dc]
        for dz in range(4) for dy in range(4) for dc in range(2)
    }
    everyone = [(planes[dx], members[dz, dy, dc]) for dx, dz, dy, dc in OFFSETS]
    peers = [members[dz, dy, dc] for dx, dz, dy, dc in OFFSETS if dx == 0]
    return everyone, peers


def kernel(
    n_member, n_state, total,
    ens_ref, obs_ref, out_ref,
    own, slab, twin, obs, part, part_in, dist, cost_ref, plan_ref, result,
    own_sems, send_sems, recv_sems, ready_sem,
):
    rows = ens_ref.shape[0]
    cols = ens_ref.shape[1] // n_member
    members = rows * n_member
    half = members // 2
    me = lax.axis_index("member")
    plane = lax.axis_index("state")
    everyone, peers = others()
    n_all = n_member * n_state
    rank = plane * n_member + me
    planes = [lax.rem(plane + step, n_state) for step in range(1, n_state)]

    barrier = pltpu.get_barrier_semaphore()
    for peer in peers:
        pl.semaphore_signal(barrier, inc=1, device_id={"member": peer}, device_id_type=MESH)
    for other in planes:
        pl.semaphore_signal(barrier, inc=1, device_id={"state": other}, device_id_type=MESH)

    def column_block(ref, index):
        return ref.at[:, pl.ds(pl.multiple_of(index * cols, cols), cols)]

    own_obs = pltpu.make_async_copy(obs_ref, obs, own_sems.at[0])
    own_obs.start()
    staged = pltpu.make_async_copy(ens_ref, own, own_sems.at[3])
    staged.start()
    far = antipode(me)
    own_block = pltpu.make_async_copy(column_block(ens_ref, me), slab.at[me], own_sems.at[1])
    own_twin = pltpu.make_async_copy(column_block(ens_ref, far), twin.at[me], own_sems.at[2])
    pl.semaphore_wait(barrier, n_member - 1 + n_state - 1)
    for other in planes:
        pl.semaphore_signal(ready_sem, inc=1, device_id={"state": other}, device_id_type=MESH)

    def send(source, target, phase, device):
        pltpu.make_async_remote_copy(
            src_ref=source,
            dst_ref=target,
            send_sem=send_sems.at[phase],
            recv_sem=recv_sems.at[phase],
            device_id=device,
            device_id_type=MESH,
        ).start()

    def wait_for(ref, sem):
        pltpu.make_async_copy(ref, ref, sem).wait()

    for peer in peers[:9]:
        send(column_block(ens_ref, peer), slab.at[me], 0, {"member": peer})
    staged.wait()
    for peer in peers[9:]:
        send(column_block(own, peer), slab.at[me], 0, {"member": peer})
    own_block.start()
    own_twin.start()

    own_obs.wait()
    raw = -2.0 * obs[...].astype(jnp.float32)
    logw = (raw - jnp.log(jnp.sum(jnp.exp(raw), axis=1, keepdims=True))) * LOG2E
    row = lax.broadcasted_iota(jnp.int32, (members, members), 0)
    column = lax.broadcasted_iota(jnp.int32, (members, members), 1)
    eye = row == column
    above = row[:half, :half] < column[:half, :half]

    own_block.wait()
    wait_for(slab.at[pl.ds(0, n_member - 1)], recv_sems.at[0])

    held = slab[...].reshape(members, cols)
    gram = lax.dot_general(
        held, held, (((1,), (1,)), ((), ())), preferred_element_type=jnp.float32
    )
    diagonal = jnp.where(eye, gram, 0.0)
    norm_col = jnp.sum(diagonal, axis=1, keepdims=True)
    norm_row = jnp.sum(diagonal, axis=0, keepdims=True)
    apart = norm_col + norm_row - 2.0 * gram
    folded = jnp.where(above, apart[:half, :half], apart[half:, half:])
    part[: n_all // 2] = folded.reshape(n_all // 2, 2, half)
    part[n_all // 2 :] = apart[:half, half:].reshape(n_all // 2, 2, half)

    pl.semaphore_wait(ready_sem, n_state - 1)
    for other, peer in everyone:
        send(
            part.at[other * n_member + peer], part_in.at[rank], 1,
            {"state": other, "member": peer},
        )
    for peer in peers[:8:-1]:
        send(column_block(own, antipode(peer)), twin.at[me], 4, {"member": peer})
    part_in[rank] = part[rank]
    wait_for(part.at[pl.ds(0, n_all - 1)], recv_sems.at[1])
    sums = jnp.sum(part_in[...].reshape(members // 8, 8, half), axis=0)
    dist[rank] = sums[0:2] + sums[2:4] + (sums[4:6] + sums[6:8])
    for other in range(n_state):
        for peer in peers:
            send(dist.at[rank], dist.at[rank], 2, {"state": other, "member": peer})

        @pl.when(plane != other)
        def _():
            send(dist.at[rank], dist.at[rank], 2, {"state": other, "member": me})

    for peer in peers[8::-1]:
        send(column_block(own, antipode(peer)), twin.at[me], 4, {"member": peer})
    wait_for(dist.at[pl.ds(0, n_all - 1)], recv_sems.at[2])

    scale_cost = 16.0 / total * LOG2E
    folded = dist[: n_all // 2].reshape(half, half) * scale_cost
    across = dist[n_all // 2 :].reshape(half, half) * scale_cost
    first = jnp.where(above, folded, 0.0)
    second = folded - first
    cost_ref[:half, :half] = first + first.T
    cost_ref[half:, half:] = second + second.T
    cost_ref[:half, half:] = across
    cost_ref[half:, :half] = across.T
    log_count = math.log2(members)

    weight = jnp.exp2(logw + LIFT)

    def two_sweeps(index, carry):
        f_pot, g_pot = carry
        scaled = jnp.exp2(g_pot + (f_pot + LIFT) - cost_ref[...])
        for again in (True, False):
            sums = jnp.sum(scaled, axis=0, keepdims=True)
            f_pot = f_pot + ((logw + LIFT) - jnp.log2(sums))
            scaled = scaled * (weight / sums)
            sums = jnp.sum(scaled, axis=1, keepdims=True)
            g_pot = g_pot + ((LIFT - log_count) - jnp.log2(sums))
            if again:
                scaled = scaled * (2.0 ** (LIFT - log_count) / sums)
        return (f_pot, g_pot)

    f_pot, g_pot = lax.fori_loop(
        0,
        SWEEPS // 2 - 1,
        two_sweeps,
        (jnp.zeros((1, members), jnp.float32), jnp.zeros((members, 1), jnp.float32)),
        unroll=3,
    )
    scaled = jnp.exp2(g_pot + (f_pot + LIFT) - cost_ref[...])
    scaled = scaled * (weight / jnp.sum(scaled, axis=0, keepdims=True))
    scaled = scaled * (2.0 ** (LIFT - log_count) / jnp.sum(scaled, axis=1, keepdims=True))
    scaled = scaled * (weight / jnp.sum(scaled, axis=0, keepdims=True))
    plan = (scaled * (1.0 / jnp.sum(scaled, axis=1, keepdims=True))).astype(jnp.bfloat16)
    n_chips = n_member // 2
    plan_ref[...] = plan.reshape(n_chips, 2 * rows, members)
    own_twin.wait()
    wait_for(twin.at[pl.ds(0, n_member - 1)], recv_sems.at[4])

    chips = near_chips()
    served = len(chips)
    core = lax.rem(me, 2)
    mine = jnp.concatenate([plan_ref[chip] for chip in chips], axis=0)
    for which, columns in enumerate((slab, twin)):
        analysis = lax.dot_general(
            mine, columns[...].reshape(members, cols), (((1,), (0,)), ((), ())),
            preferred_element_type=jnp.float32,
        )
        result[which] = analysis.reshape(2 * served, rows, cols).astype(jnp.bfloat16)

    def serve(place):
        for which, owner in enumerate((me, far)):
            target = column_block(out_ref, owner)
            if place < served - 1:
                for side in range(2):
                    send(
                        result.at[which, 2 * place + side], target, 3,
                        {"member": chips[place] * 2 + side},
                    )
            else:
                send(
                    result.at[which, 2 * place + 1 - core], target, 3, {"member": me + 1 - 2 * core}
                )

    for turn in range(4):
        for place in range(served):
            pl.when(lax.div(chips[place], 4) == turn)(functools.partial(serve, place))
    own_sets = [
        pltpu.make_async_copy(
            result.at[which, 2 * (served - 1) + core], column_block(out_ref, owner), own_sems.at[1 + which]
        )
        for which, owner in enumerate((me, far))
    ]
    for copy in own_sets:
        copy.start()

    wait_for(slab.at[pl.ds(0, n_member - 1)], send_sems.at[0])
    wait_for(part.at[pl.ds(0, n_all - 1)], send_sems.at[1])
    wait_for(dist.at[pl.ds(0, n_all - 1)], send_sems.at[2])
    wait_for(twin.at[pl.ds(0, n_member - 1)], send_sems.at[4])
    for copy in own_sets:
        copy.wait()
    wait_for(out_ref.at[:, pl.ds(0, (n_member - 2) * cols)], send_sems.at[3])
    wait_for(out_ref.at[:, pl.ds(0, (n_member - 2) * cols)], recv_sems.at[3])


def per_device(n_member, n_state, ensemble, obs_count):
    rows, width = ensemble.shape
    members, cols = rows * n_member, width // n_member
    half, n_all = members // 2, n_member * n_state
    return pl.pallas_call(
        functools.partial(kernel, n_member, n_state, width * n_state),
        out_shape=jax.ShapeDtypeStruct((rows, width), jnp.bfloat16),
        in_specs=[pl.BlockSpec(memory_space=pl.ANY), pl.BlockSpec(memory_space=pl.ANY)],
        out_specs=pl.BlockSpec(memory_space=pl.ANY),
        scratch_shapes=[
            pltpu.VMEM((rows, width), jnp.bfloat16),
            pltpu.VMEM((n_member, rows, cols), jnp.bfloat16),
            pltpu.VMEM((n_member, rows, cols), jnp.bfloat16),
            pltpu.VMEM((1, members), jnp.int32),
            pltpu.VMEM((n_all, 2, half), jnp.float32),
            pltpu.VMEM((n_all, 2, half), jnp.float32),
            pltpu.VMEM((n_all, 2, half), jnp.float32),
            pltpu.VMEM((members, members), jnp.float32),
            pltpu.VMEM((n_member // 2, 2 * rows, members), jnp.bfloat16),
            pltpu.VMEM((2, n_member // 2, rows, cols), jnp.bfloat16),
            pltpu.SemaphoreType.DMA((4,)),
            pltpu.SemaphoreType.DMA((5,)),
            pltpu.SemaphoreType.DMA((5,)),
            pltpu.SemaphoreType.REGULAR,
        ],
        compiler_params=pltpu.CompilerParams(
            collective_id=0, has_side_effects=True, vmem_limit_bytes=53 * 1024 * 1024
        ),
    )(
        pltpu.with_memory_space_constraint(ensemble, pltpu.HBM),
        pltpu.with_memory_space_constraint(obs_count.reshape(1, members), pltpu.HBM),
    )


def solution(mesh):
    body = functools.partial(per_device, mesh.shape["member"], mesh.shape["state"])
    return jax.shard_map(
        body, mesh=mesh, in_specs=(P("member", "state"), P()), out_specs=P("member", "state"),
        check_vma=False,
    )
```
